256 devices in a mesh: graph: 16 (over z, core), feat: 16 (over y, x).
Axes of the slice: x: 4, y: 4, z: 8, core: 2. Of those that a mesh axis runs over, the one named last changes fastest.
Arguments:
- features: bfloat16 [131072, 768], P('graph', 'feat'), may hold values from -6 to 6
- frontier_ids: int32 [16, 16, 512], P('graph'), may hold values from 0 to 8191
- self_one_ids: int32 [16, 2048], P('graph'), may hold values from 0 to 8191
- neigh_one_ids: int32 [16, 16, 2048], P('graph'), may hold values from 0 to 8191
- count_one: int32 [16, 2048], P('graph'), may hold values from 1 to 16, as said below
- self_two_ids: int32 [16, 1536], P('graph', 'feat'), may hold values from 0 to 2047
- neigh_two_ids: int32 [16, 16, 1536], P('graph', None, 'feat'), may hold values from 0 to 2047
- count_two: int32 [16, 1536], P('graph', 'feat'), may hold values from 1 to 16, as said below
- pos_pairs: int32 [16, 2, 512], P('graph', None, 'feat'), may hold values from 0 to 1535
- neg_ids: int32 [16, 512], P('graph'), may hold values from 0 to 1535
- first_self: bfloat16 [768, 256], P('feat'), may hold values from -0.21875 to 0.21875
- first_neigh: bfloat16 [768, 256], P('feat'), may hold values from -0.21875 to 0.21875
- second_self: bfloat16 [256, 256], replicated, may hold values from -0.25 to 0.25
- second_neigh: bfloat16 [256, 256], replicated, may hold values from -0.25 to 0.25
Outputs:
- grad_first_self: float32 [768, 256], P('feat')
- grad_first_neigh: float32 [768, 256], P('feat')
- grad_second_self: float32 [256, 256], replicated
- grad_second_neigh: float32 [256, 256], replicated
- mean_loss: float32 [], replicated
The draws below stay inside these ranges and needn't reach their ends.
Inputs may be any that keep to these rules, and one draw needn't show every extreme that they name: `frontier_ids`: row of owner o's block of 8192 nodes that group g asks for in slot s. `neigh_one_ids`: only the first count_one[g, i] of the 16 slots are live. `count_one`: every group has a first-hop node with 16 live neighbours. `neigh_two_ids`: only the first count_two[g, t] of the 16 slots are live. `count_two`: every group has a target with 16 live neighbours.
All inputs are finite; a program needn't handle non-finite values.
Results may differ from the reference program's by a relative error of at most 0.025.
Values may be sent and summed in bfloat16 or wider, within the bound.
No kernel may reach another device: no remote copies, remote signals or barrier semaphores. Data moves between devices by JAX's collectives and lax.ppermute only.
A program may use at most 64 MiB of HBM per device.

```python
import math
import jax
import jax.numpy as jnp
from jax import lax

D = 768
H = 256
FAN = 16
ROWS_DEV = 8192
CAP = 512
NODES = 131072
FRONT = 8192
PAIRS = 512
NEG = 512
TGT = 1536
HOP1 = 2048
N_GRAPH = 16


def count_draw(key, row_total):
    picked = jax.random.randint(key, (N_GRAPH, row_total), 1, FAN + 1)
    full_at = jax.random.randint(jax.random.fold_in(key, 7), (N_GRAPH, 1), 0, row_total)
    marks = jnp.arange(row_total, dtype=jnp.int32)[None, :] == full_at
    return jnp.where(marks, FAN, picked).astype(jnp.int32)


def draw_count_one(key, part):
    key = jax.random.fold_in(key, 1)
    return count_draw(key, HOP1)


def draw_count_two(key, part):
    key = jax.random.fold_in(key, 2)
    return count_draw(key, TGT)


def place_ends(drawn, key, least, largest):
    dims = drawn.shape
    spot = [jax.random.randint(jax.random.fold_in(key, axis), (), 0, dims[axis]) for axis in range(len(dims))]
    drawn = drawn.at[tuple(spot)].set(least)
    longest = dims.index(max(dims))
    spot[longest] = (spot[longest] + 1) % dims[longest]
    return drawn.at[tuple(spot)].set(largest)


def shard_levels(rng, dims, pieces, least, top_value):
    factor_of = 1.0
    for axis_at, shards_of in pieces:
        steps = jax.random.uniform(jax.random.fold_in(jax.random.fold_in(rng, 6), axis_at), (shards_of,), jnp.float32, least / len(pieces), top_value / len(pieces))
        factor_of = factor_of * jnp.repeat(jnp.exp(steps), dims[axis_at] // shards_of).reshape((-1,) + (1,) * (len(dims) - 1 - axis_at))
    return factor_of


def noise(stream_key, shape, scale, most, shards=(), kind=jnp.bfloat16):
    values = scale * jax.random.normal(stream_key, shape, jnp.float32)
    if shards:
        values = values * shard_levels(stream_key, shape, shards, -0.22, 0.18)
    return jnp.clip(values, -most, most).astype(kind)


def setup_inputs(seed: int = 0) -> dict:
    streams_of = jax.random.split(jax.random.key(seed), 15)
    return {
        "features": noise(streams_of[0], (NODES, D), 1.0, 6.0, ((0, 16), (1, 16))),
        "frontier_ids": place_ends(jax.random.randint(streams_of[1], (N_GRAPH, N_GRAPH, CAP), 0, ROWS_DEV), jax.random.fold_in(streams_of[1], 1), 0, ROWS_DEV - 1).astype(jnp.int32),
        "self_one_ids": place_ends(jax.random.randint(streams_of[2], (N_GRAPH, HOP1), 0, FRONT), jax.random.fold_in(streams_of[2], 1), 0, FRONT - 1).astype(jnp.int32),
        "neigh_one_ids": place_ends(jax.random.randint(streams_of[3], (N_GRAPH, FAN, HOP1), 0, FRONT), jax.random.fold_in(streams_of[3], 1), 0, FRONT - 1).astype(jnp.int32),
        "count_one": draw_count_one(jax.random.fold_in(streams_of[14], 71), 0),
        "self_two_ids": place_ends(jax.random.randint(streams_of[5], (N_GRAPH, TGT), 0, HOP1), jax.random.fold_in(streams_of[5], 1), 0, HOP1 - 1).astype(jnp.int32),
        "neigh_two_ids": place_ends(jax.random.randint(streams_of[6], (N_GRAPH, FAN, TGT), 0, HOP1), jax.random.fold_in(streams_of[6], 1), 0, HOP1 - 1).astype(jnp.int32),
        "count_two": draw_count_two(jax.random.fold_in(streams_of[14], 71), 0),
        "pos_pairs": place_ends(jax.random.randint(streams_of[8], (N_GRAPH, 2, PAIRS), 0, TGT), jax.random.fold_in(streams_of[8], 1), 0, TGT - 1).astype(jnp.int32),
        "neg_ids": place_ends(jax.random.randint(streams_of[9], (N_GRAPH, NEG), 0, TGT), jax.random.fold_in(streams_of[9], 1), 0, TGT - 1).astype(jnp.int32),
        "first_self": noise(streams_of[10], (D, H), D ** -0.5, 0.21875, ((0, 16),)),
        "first_neigh": noise(streams_of[11], (D, H), D ** -0.5, 0.21875, ((0, 16),)),
        "second_self": noise(streams_of[12], (H, H), (0.25 * H ** -0.5), 0.25),
        "second_neigh": noise(streams_of[13], (H, H), (0.25 * H ** -0.5), 0.25),
    }


def neighbour_mean(source, neigh_ids, counts):
    running = jnp.zeros((neigh_ids.shape[1], source.shape[1]), jnp.float32)
    for position in range(neigh_ids.shape[0]):
        picked = jnp.take(source, neigh_ids[position], axis=0).astype(jnp.float32)
        running = running + jnp.where((position < counts)[:, None], picked, 0.0)
    return (running / counts.astype(jnp.float32)[:, None]).astype(jnp.bfloat16)

def spread_back(grad_rows, neigh_ids, counts, row_total):
    weights = 1.0 / counts.astype(jnp.float32)
    result = jnp.zeros((row_total, grad_rows.shape[1]), jnp.float32)
    for position in range(neigh_ids.shape[0]):
        scaled = jnp.where((position < counts)[:, None], grad_rows * weights[:, None], 0.0)
        result = result.at[neigh_ids[position]].add(scaled)
    return result

def contract_rows(former, latter):
    return lax.dot_general(former, latter, (((0,), (0,)), ((), ())), preferred_element_type=jnp.float32)

def contract_cols(former, latter):
    return lax.dot_general(former, latter, (((1,), (1,)), ((), ())), preferred_element_type=jnp.float32)

def reference(features, frontier_ids, self_one_ids, neigh_one_ids, count_one, self_two_ids, neigh_two_ids, count_two, pos_pairs, neg_ids, first_self, first_neigh, second_self, second_neigh):
    scale = 1.0 / math.sqrt(H)
    owners = (jnp.arange(N_GRAPH, dtype=jnp.int32) * ROWS_DEV)[:, None]
    grad_fs = jnp.zeros((D, H), jnp.float32)
    grad_fn = jnp.zeros((D, H), jnp.float32)
    grad_ss = jnp.zeros((H, H), jnp.float32)
    grad_sn = jnp.zeros((H, H), jnp.float32)
    total = jnp.zeros((), jnp.float32)
    for group in range(N_GRAPH):
        frontier = jnp.take(features, (frontier_ids[group] + owners).reshape(-1).astype(jnp.int32), axis=0)
        self_rows = jnp.take(frontier, self_one_ids[group], axis=0)
        neigh_rows = neighbour_mean(frontier, neigh_one_ids[group], count_one[group])
        hidden_pre = jnp.dot(self_rows, first_self, preferred_element_type=jnp.float32) + jnp.dot(neigh_rows, first_neigh, preferred_element_type=jnp.float32)
        hidden = jnp.maximum(hidden_pre, 0.0).astype(jnp.bfloat16)
        hidden_self = jnp.take(hidden, self_two_ids[group], axis=0)
        hidden_neigh = neighbour_mean(hidden, neigh_two_ids[group], count_two[group])
        embed = (jnp.dot(hidden_self, second_self, preferred_element_type=jnp.float32) + jnp.dot(hidden_neigh, second_neigh, preferred_element_type=jnp.float32)).astype(jnp.bfloat16)
        sources = pos_pairs[group, 0]
        targets = pos_pairs[group, 1]
        negatives = neg_ids[group]
        source_rows = jnp.take(embed, sources, axis=0)
        dest_rows = jnp.take(embed, targets, axis=0)
        negative_rows = jnp.take(embed, negatives, axis=0)
        pos_score = lax.optimization_barrier(jnp.sum(source_rows.astype(jnp.float32) * dest_rows.astype(jnp.float32), axis=1)) * scale
        neg_score = contract_cols(source_rows, negative_rows) * scale
        total = total + jnp.sum(jax.nn.softplus(-pos_score)) + jnp.sum(jax.nn.softplus(neg_score)) / NEG
        pos_grad = -jax.nn.sigmoid(-pos_score)
        neg_grad = (jax.nn.sigmoid(neg_score) / NEG).astype(jnp.bfloat16)
        source_grad = (pos_grad[:, None] * dest_rows.astype(jnp.float32) + jnp.dot(neg_grad, negative_rows, preferred_element_type=jnp.float32)) * scale
        dest_grad = pos_grad[:, None] * source_rows.astype(jnp.float32) * scale
        negative_grad = contract_rows(neg_grad, source_rows) * scale
        embed_grad = jnp.zeros((TGT, H), jnp.float32)
        embed_grad = embed_grad.at[sources].add(source_grad).at[targets].add(dest_grad).at[negatives].add(negative_grad)
        embed_grad = embed_grad.astype(jnp.bfloat16)
        grad_ss = grad_ss + contract_rows(hidden_self, embed_grad)
        grad_sn = grad_sn + contract_rows(hidden_neigh, embed_grad)
        self_back = contract_cols(embed_grad, second_self)
        neigh_back = contract_cols(embed_grad, second_neigh)
        hidden_grad = jnp.zeros((HOP1, H), jnp.float32).at[self_two_ids[group]].add(self_back)
        hidden_grad = hidden_grad + spread_back(neigh_back, neigh_two_ids[group], count_two[group], HOP1)
        pre_grad = jnp.where(hidden_pre > 0, hidden_grad, 0.0).astype(jnp.bfloat16)
        grad_fs = grad_fs + contract_rows(self_rows, pre_grad)
        grad_fn = grad_fn + contract_rows(neigh_rows, pre_grad)
    return (grad_fs, grad_fn, grad_ss, grad_sn, total / (PAIRS * N_GRAPH))
```

```python
import functools
import math

import jax
import jax.numpy as jnp
from jax import lax
from jax.experimental import pallas as pl
from jax.experimental.pallas import tpu as pltpu
from jax.sharding import PartitionSpec as P

BF = jnp.bfloat16
F32 = jnp.float32
VMEM_LIMIT = 48 * 2**20


def swap(value, axis):
    return lax.all_to_all(value, axis, split_axis=0, concat_axis=0, tiled=True)


def gather_all(value, axis):
    size = lax.axis_size(axis)
    return swap(jnp.broadcast_to(value[None], (size,) + value.shape), axis)


def dot(former, latter, dims):
    return lax.dot_general(former, latter, (dims, ((), ())), preferred_element_type=F32)


def serve_kernel(ids_ref, feat_ref, out_ref, table, picked):
    width, rows = feat_ref.shape
    groups, _, cap = out_ref.shape
    step = 512

    def fill(at, _):
        at = pl.multiple_of(at * step, step)
        table[pl.ds(at, step), 0:width] = feat_ref[:, pl.ds(at, step)].astype(F32).T
        return 0

    lax.fori_loop(0, rows // step, fill, 0)

    def per_group(group, _):
        base = group * cap

        def pick(at, _):
            for lane in range(32):
                row = at * 32 + lane
                picked[pl.ds(row, 1), :] = table[pl.ds(ids_ref[base + row], 1), :]
            return 0

        lax.fori_loop(0, cap // 32, pick, 0)
        out_ref[group] = picked[:, 0:width].T.astype(out_ref.dtype)
        return 0

    lax.fori_loop(0, groups, per_group, 0)


def serve(features_t, ids, groups, cap):
    width, rows = features_t.shape
    return pl.pallas_call(
        serve_kernel,
        out_shape=jax.ShapeDtypeStruct((groups, width, cap), features_t.dtype),
        in_specs=[
            pl.BlockSpec(memory_space=pltpu.SMEM),
            pl.BlockSpec(memory_space=pltpu.VMEM),
        ],
        out_specs=pl.BlockSpec(memory_space=pltpu.VMEM),
        scratch_shapes=[pltpu.VMEM((rows, 128), F32), pltpu.VMEM((cap, 128), F32)],
        compiler_params=pltpu.CompilerParams(vmem_limit_bytes=VMEM_LIMIT),
        name="serve",
    )(ids, features_t)


def hop_kernel(fan, ids_ref, self_ref, front_ref, inv_ref, out_ref, table, own, total):
    owners, width, cap = front_ref.shape
    nodes = out_ref.shape[0] * out_ref.shape[2]
    block = out_ref.shape[2]

    def fill(owner, _):
        at = pl.multiple_of(owner * cap, cap)
        table[pl.ds(at, cap), 0:width] = front_ref[owner].astype(F32).T
        return 0

    lax.fori_loop(0, owners, fill, 0)
    table[pl.ds(owners * cap, 8), :] = jnp.zeros((8, 128), F32)

    def per_block(dest, _):
        base = dest * block

        def pick(at, _):
            for lane in range(8):
                row = at * 8 + lane
                node = base + row
                rows = [
                    table[pl.ds(ids_ref[node * fan + slot], 1), :] for slot in range(fan)
                ]
                while len(rows) > 1:
                    rows = [rows[at] + rows[at + 1] for at in range(0, len(rows), 2)]
                total[pl.ds(row, 1), :] = rows[0]
                own[pl.ds(row, 1), :] = table[pl.ds(self_ref[node], 1), :]
            return 0

        lax.fori_loop(0, block // 8, pick, 0)
        out_ref[dest, 0:width, :] = own[:, 0:width].T.astype(out_ref.dtype)
        inv = inv_ref[pl.ds(dest, 1), :]
        out_ref[dest, width : 2 * width, :] = (total[:, 0:width].T * inv).astype(out_ref.dtype)
        return 0

    lax.fori_loop(0, out_ref.shape[0], per_block, 0)


def hop(frontier, ids, self_ids, inv, blocks):
    owners, width, cap = frontier.shape
    nodes = self_ids.shape[0]
    fan = ids.shape[0] // nodes
    block = nodes // blocks
    return pl.pallas_call(
        functools.partial(hop_kernel, fan),
        out_shape=jax.ShapeDtypeStruct((blocks, 2 * width, block), frontier.dtype),
        in_specs=[
            pl.BlockSpec(memory_space=pltpu.SMEM),
            pl.BlockSpec(memory_space=pltpu.SMEM),
            pl.BlockSpec(memory_space=pltpu.VMEM),
            pl.BlockSpec(memory_space=pltpu.VMEM),
        ],
        out_specs=pl.BlockSpec(memory_space=pltpu.VMEM),
        scratch_shapes=[
            pltpu.VMEM((owners * cap + 8, 128), F32),
            pltpu.VMEM((block, 128), F32),
            pltpu.VMEM((block, 128), F32),
        ],
        compiler_params=pltpu.CompilerParams(vmem_limit_bytes=VMEM_LIMIT),
        name="first_hop",
    )(ids, self_ids, frontier, inv)


def one_hot(ids, total):
    marks = lax.broadcasted_iota(jnp.int32, (ids.shape[0], total), 1)
    return (ids[:, None] == marks).astype(BF)


def count_hot(ids, counts, total):
    marks = lax.broadcasted_iota(jnp.int32, (ids.shape[1], total), 1)
    result = jnp.zeros((ids.shape[1], total), F32)
    for slot in range(ids.shape[0]):
        live = jnp.where(slot < counts, ids[slot], -1)
        result = result + (live[:, None] == marks).astype(F32)
    return result.astype(BF)


def local(
    features,
    frontier_ids,
    self_one_ids,
    neigh_one_ids,
    count_one,
    self_two_ids,
    neigh_two_ids,
    count_two,
    pos_pairs,
    neg_ids,
    first_self,
    first_neigh,
    second_self,
    second_neigh,
):
    graphs = lax.axis_size("graph")
    feats = lax.axis_size("feat")
    hidden_width = second_self.shape[0]
    scale = 1.0 / math.sqrt(hidden_width)
    negative_total = neg_ids.shape[1]
    nodes = self_one_ids.shape[1]
    fan = neigh_one_ids.shape[1]
    width = features.shape[1]
    cap = frontier_ids.shape[2]
    front = graphs * cap
    share = self_two_ids.shape[1]
    pair_share = pos_pairs.shape[2]

    asked = swap(frontier_ids[0], "graph")
    weights = gather_all(jnp.concatenate([first_self, first_neigh], axis=0), "feat")
    packed = jnp.concatenate(
        [
            self_two_ids[0],
            count_two[0],
            neigh_two_ids[0].reshape(-1),
            pos_pairs[0].reshape(-1),
        ]
    )
    packed = gather_all(packed, "feat")
    self_two = packed[:, :share].reshape(-1)
    counts_two = packed[:, share : 2 * share].reshape(-1)
    neigh_two = packed[:, 2 * share : (2 + fan) * share].reshape(feats, fan, share)
    neigh_two = neigh_two.transpose(1, 0, 2).reshape(fan, -1)
    pairs = packed[:, (2 + fan) * share :].reshape(feats, 2, pair_share)
    pairs = pairs.transpose(1, 0, 2).reshape(2, -1)
    targets_total = self_two.shape[0]

    slots = lax.broadcasted_iota(jnp.int32, (fan, nodes), 0)
    live_ids = jnp.where(slots < count_one, neigh_one_ids[0], front).T.reshape(-1)
    inv_one = (1.0 / count_one.astype(F32)).reshape(feats, -1)

    served = serve(features.T, asked.reshape(-1), graphs, cap)
    frontier = swap(served, "graph")
    rows_one = hop(frontier, live_ids, self_one_ids[0], inv_one, feats)
    mine = swap(rows_one, "feat")
    hidden_pre = dot(
        mine.reshape(feats * 2 * width, -1),
        weights.reshape(feats * 2 * width, hidden_width),
        ((0,), (0,)),
    )
    hidden = gather_all(jnp.maximum(hidden_pre, 0.0).astype(BF), "feat")
    hidden = hidden.reshape(nodes, hidden_width)

    pick_self = one_hot(self_two, nodes)
    pick_neigh = count_hot(neigh_two, counts_two, nodes)
    inv_two = (1.0 / counts_two.astype(F32))[:, None]
    hidden_self = dot(pick_self, hidden, ((1,), (0,))).astype(BF)
    hidden_neigh = (dot(pick_neigh, hidden, ((1,), (0,))) * inv_two).astype(BF)
    embed = (
        dot(hidden_self, second_self, ((1,), (0,)))
        + dot(hidden_neigh, second_neigh, ((1,), (0,)))
    ).astype(BF)

    pair_total = pairs.shape[1]
    ends = jnp.concatenate([pairs[0], pairs[1], neg_ids[0]])
    pick_ends = one_hot(ends, targets_total)
    end_rows = dot(pick_ends, embed, ((1,), (0,))).astype(BF)
    source_rows = end_rows[:pair_total]
    dest_rows = end_rows[pair_total : 2 * pair_total]
    negative_rows = end_rows[2 * pair_total :]
    pos_score = (
        jnp.sum(source_rows.astype(F32) * dest_rows.astype(F32), axis=1, keepdims=True) * scale
    )
    neg_score = dot(source_rows, negative_rows, ((1,), (1,))) * scale
    loss_part = (
        jnp.sum(jax.nn.softplus(-pos_score)) + jnp.sum(jax.nn.softplus(neg_score)) / negative_total
    )
    pos_grad = -jax.nn.sigmoid(-pos_score)
    neg_grad = (jax.nn.sigmoid(neg_score) / negative_total).astype(BF)
    source_grad = (
        pos_grad * dest_rows.astype(F32) + dot(neg_grad, negative_rows, ((1,), (0,)))
    ) * scale
    dest_grad = pos_grad * source_rows.astype(F32) * scale
    negative_grad = dot(neg_grad, source_rows, ((0,), (0,))) * scale
    end_grads = jnp.concatenate([source_grad, dest_grad, negative_grad]).astype(BF)
    embed_grad = dot(pick_ends, end_grads, ((0,), (0,))).astype(BF)

    grad_ss = dot(hidden_self, embed_grad, ((0,), (0,)))
    grad_sn = dot(hidden_neigh, embed_grad, ((0,), (0,)))
    self_back = dot(embed_grad, second_self, ((1,), (1,))).astype(BF)
    neigh_back = (dot(embed_grad, second_neigh, ((1,), (1,))) * inv_two).astype(BF)
    hidden_grad = dot(pick_self, self_back, ((0,), (0,))) + dot(
        pick_neigh, neigh_back, ((0,), (0,))
    )
    pre_grad = jnp.where(hidden > 0, hidden_grad, 0.0).astype(BF)
    first_part = dot(
        rows_one.transpose(1, 0, 2).reshape(2 * width, nodes), pre_grad, ((1,), (0,))
    )

    loss_high = loss_part.astype(BF)
    loss_mid = (loss_part - loss_high.astype(F32)).astype(BF)
    loss_low = (loss_part - loss_high.astype(F32) - loss_mid.astype(F32)).astype(BF)
    loss_row = jnp.zeros((graphs, 1, hidden_width), BF)
    loss_row = loss_row.at[:, 0, 0].set(loss_high).at[:, 0, 1].set(loss_mid)
    loss_row = loss_row.at[:, 0, 2].set(loss_low)
    parts = jnp.concatenate(
        [
            first_part.astype(BF).reshape(graphs, -1, hidden_width),
            grad_ss.astype(BF).reshape(graphs, -1, hidden_width),
            grad_sn.astype(BF).reshape(graphs, -1, hidden_width),
            loss_row,
        ],
        axis=1,
    )
    sums = jnp.sum(swap(parts, "graph").astype(F32), axis=0)
    loss = jnp.sum(sums[-1, 0:3])
    first_rows = 2 * width // graphs
    second_rows = hidden_width // graphs
    whole = gather_all(sums[:-1].astype(BF), "graph").astype(F32)
    first_sums = whole[:, :first_rows].reshape(2 * width, hidden_width)
    ss = whole[:, first_rows : first_rows + second_rows].reshape(hidden_width, hidden_width)
    sn = whole[:, first_rows + second_rows :].reshape(hidden_width, hidden_width)
    return (
        first_sums[:width],
        first_sums[width:],
        ss,
        sn,
        loss / (pair_total * graphs),
    )


def solution(mesh):
    placed = (
        P("graph", "feat"),
        P("graph", None, None),
        P("graph", None),
        P("graph", None, None),
        P("graph", None),
        P("graph", "feat"),
        P("graph", None, "feat"),
        P("graph", "feat"),
        P("graph", None, "feat"),
        P("graph", None),
        P("feat", None),
        P("feat", None),
        P(),
        P(),
    )
    return jax.shard_map(
        local,
        mesh=mesh,
        in_specs=placed,
        out_specs=(P("feat", None), P("feat", None), P(), P(), P()),
        check_vma=False,
    )
```

```python
import functools
import math

import jax
import jax.numpy as jnp
from jax import lax
from jax.experimental import pallas as pl
from jax.experimental.pallas import tpu as pltpu
from jax.sharding import PartitionSpec as P

BF = jnp.bfloat16
F32 = jnp.float32
VMEM_LIMIT = 48 * 2**20


def swap(value, axis):
    return lax.all_to_all(value, axis, split_axis=0, concat_axis=0, tiled=True)


def gather_all(value, axis):
    size = lax.axis_size(axis)
    return swap(jnp.broadcast_to(value[None], (size,) + value.shape), axis)


def dot(former, latter, dims):
    return lax.dot_general(former, latter, (dims, ((), ())), preferred_element_type=F32)


def serve_kernel(ids_ref, feat_ref, out_ref, table, picked):
    width, rows = feat_ref.shape
    groups, _, cap = out_ref.shape
    step = 512

    def fill(at, _):
        at = pl.multiple_of(at * step, step)
        table[pl.ds(at, step), 0:width] = feat_ref[:, pl.ds(at, step)].astype(F32).T
        return 0

    lax.fori_loop(0, rows // step, fill, 0)

    def per_group(group, _):
        base = group * cap

        def pick(at, _):
            for lane in range(32):
                row = at * 32 + lane
                picked[pl.ds(row, 1), :] = table[pl.ds(ids_ref[base + row], 1), :]
            return 0

        lax.fori_loop(0, cap // 32, pick, 0)
        out_ref[group] = picked[:, 0:width].T.astype(out_ref.dtype)
        return 0

    lax.fori_loop(0, groups, per_group, 0)


def serve(features_t, ids, groups, cap):
    width, rows = features_t.shape
    return pl.pallas_call(
        serve_kernel,
        out_shape=jax.ShapeDtypeStruct((groups, width, cap), features_t.dtype),
        in_specs=[
            pl.BlockSpec(memory_space=pltpu.SMEM),
            pl.BlockSpec(memory_space=pltpu.VMEM),
        ],
        out_specs=pl.BlockSpec(memory_space=pltpu.VMEM),
        scratch_shapes=[pltpu.VMEM((rows, 128), F32), pltpu.VMEM((cap, 128), F32)],
        compiler_params=pltpu.CompilerParams(vmem_limit_bytes=VMEM_LIMIT),
        name="serve",
    )(ids, features_t)


def count_kernel(keys_ref, lows_ref, out_ref, marks):
    chunks, _, chunk = out_ref.shape
    spans = chunks * chunk // 256
    across = chunk // 256

    @pl.when(pl.program_id(0) == 0)
    def _():
        marks[...] = lax.broadcasted_iota(jnp.int32, (256, 256), 0).astype(F32).astype(BF)

    def stretch(row, rows):
        small = jnp.broadcast_to(row, (16, 256)).astype(BF)
        return jnp.concatenate([small] * (rows // 16), axis=0)

    def block(at, _):
        one = jnp.ones((256, 256), BF)
        zero = jnp.zeros((256, 256), BF)
        low = stretch(lows_ref[pl.ds(at, 1), :], 256)
        right = jnp.where(low == marks[...], one, zero)
        place = pl.multiple_of(at * 16, 16)
        for first in range(0, spans, 16):
            size = min(16, spans - first)
            key = stretch(keys_ref[pl.ds(at, 1), :] - float(first * 16), size * 16)
            left = jnp.where(key == marks[0 : size * 16, :], one[: size * 16], zero[: size * 16])
            part = dot(left, right, ((1,), (1,))).astype(BF)
            for inner in range(size):
                span = first + inner
                lane = (span % across) * 256
                out_ref[span // across, pl.ds(place, 16), lane : lane + 256] = part[
                    inner * 16 : (inner + 1) * 16
                ]
        return 0

    lax.fori_loop(0, 16, block, 0, unroll=8)


def count_matrix(highs, lows, total, chunk):
    fan, nodes = highs.shape

    def order(value):
        return value.reshape(fan, nodes // 16, 16).transpose(1, 0, 2).reshape(nodes // 16, -1)

    node = (lax.broadcasted_iota(jnp.int32, (fan, nodes), 1) % 16).astype(F32)
    keys = order(highs * 16.0 + node)
    return pl.pallas_call(
        count_kernel,
        grid=(nodes // 256,),
        out_shape=jax.ShapeDtypeStruct((total // chunk, nodes, chunk), BF),
        in_specs=[
            pl.BlockSpec((16, 256), lambda at: (at, 0)),
            pl.BlockSpec((16, 256), lambda at: (at, 0)),
        ],
        out_specs=pl.BlockSpec((total // chunk, 256, chunk), lambda at: (0, at, 0)),
        scratch_shapes=[pltpu.VMEM((256, 256), BF)],
        compiler_params=pltpu.CompilerParams(vmem_limit_bytes=VMEM_LIMIT),
        cost_estimate=pl.CostEstimate(
            flops=2 * nodes * total * 256 // 16 * 16,
            bytes_accessed=2 * nodes * total,
            transcendentals=0,
        ),
        name="count_matrix",
    )(keys, order(lows))


def hop_kernel(self_ref, counts_ref, front_ref, inv_ref, out_ref, table, total, own):
    owners, width, cap = front_ref.shape
    blocks, _, block = out_ref.shape
    step = pl.program_id(0)
    parts = []
    for owner in range(owners):
        rows = front_ref[owner].astype(F32).T
        at = pl.multiple_of((step * owners + owner) * cap, cap)
        table[pl.ds(at, cap), 0:width] = rows
        parts.append(rows.astype(BF))
    part = dot(counts_ref[0], jnp.concatenate(parts, axis=0), ((1,), (0,)))

    @pl.when(step == 0)
    def _():
        total[...] = part

    @pl.when(step > 0)
    def _():
        total[...] += part

    @pl.when(step == pl.num_programs(0) - 1)
    def _():
        def per_block(dest, _):
            base = pl.multiple_of(dest * block, block)

            def pick(at, _):
                for lane in range(32):
                    row = at * 32 + lane
                    own[pl.ds(row, 1), :] = table[pl.ds(self_ref[base + row], 1), :]
                return 0

            lax.fori_loop(0, block // 32, pick, 0)
            out_ref[dest, 0:width, :] = own[:, 0:width].T.astype(BF)
            mean = total[pl.ds(base, block), :].T * inv_ref[pl.ds(dest, 1), :]
            out_ref[dest, width : 2 * width, :] = mean.astype(BF)
            return 0

        lax.fori_loop(0, blocks, per_block, 0)


def hop(frontier, counts, self_ids, inv, blocks):
    owners, width, cap = frontier.shape
    chunks, nodes, chunk = counts.shape
    block = nodes // blocks
    per = chunk // cap
    return pl.pallas_call(
        hop_kernel,
        grid=(chunks,),
        out_shape=jax.ShapeDtypeStruct((blocks, 2 * width, block), BF),
        in_specs=[
            pl.BlockSpec(memory_space=pltpu.SMEM),
            pl.BlockSpec((1, nodes, chunk), lambda at: (at, 0, 0)),
            pl.BlockSpec((per, width, cap), lambda at: (at, 0, 0)),
            pl.BlockSpec(inv.shape, lambda at: (0, 0)),
        ],
        out_specs=pl.BlockSpec((blocks, 2 * width, block), lambda at: (0, 0, 0)),
        scratch_shapes=[
            pltpu.VMEM((owners * cap, 128), F32),
            pltpu.VMEM((nodes, width), F32),
            pltpu.VMEM((block, 128), F32),
        ],
        compiler_params=pltpu.CompilerParams(vmem_limit_bytes=VMEM_LIMIT),
        cost_estimate=pl.CostEstimate(
            flops=2 * nodes * chunks * chunk * 128,
            bytes_accessed=2 * nodes * chunks * chunk,
            transcendentals=0,
        ),
        name="first_hop",
    )(self_ids, counts, frontier, inv)


def one_hot(ids, total):
    marks = lax.broadcasted_iota(jnp.int32, (ids.shape[0], total), 1)
    return (ids[:, None] == marks).astype(BF)


def halves(ids):
    return (ids // 256).astype(F32), (ids % 256).astype(F32)


def local(
    features,
    frontier_ids,
    self_one_ids,
    neigh_one_ids,
    count_one,
    self_two_ids,
    neigh_two_ids,
    count_two,
    pos_pairs,
    neg_ids,
    first_self,
    first_neigh,
    second_self,
    second_neigh,
):
    graphs = lax.axis_size("graph")
    feats = lax.axis_size("feat")
    hidden_width = second_self.shape[0]
    scale = 1.0 / math.sqrt(hidden_width)
    negative_total = neg_ids.shape[1]
    nodes = self_one_ids.shape[1]
    fan = neigh_one_ids.shape[1]
    width = features.shape[1]
    cap = frontier_ids.shape[2]
    front = graphs * cap
    share = self_two_ids.shape[1]
    pair_share = pos_pairs.shape[2]

    asked = swap(frontier_ids[0], "graph")

    slots = lax.broadcasted_iota(jnp.int32, (fan, 1), 0)
    neigh_high, neigh_low = halves(neigh_two_ids[0])
    neigh_low = jnp.where(slots < count_two, neigh_low, -1.0)
    fields = [*halves(self_two_ids), count_two.astype(F32), neigh_high, neigh_low]
    fields = [field.reshape(-1) for field in fields + list(halves(pos_pairs[0]))]
    field_sizes = [field.shape[0] for field in fields]
    spare = -sum(field_sizes) % (16 * hidden_width)
    fields = jnp.concatenate(fields + [jnp.zeros((spare,), F32)]).astype(BF)
    early = jnp.concatenate(
        [first_self, first_neigh, fields.reshape(-1, hidden_width)], axis=0
    )
    early = gather_all(early, "feat")

    served = serve(features.T, asked.reshape(-1), graphs, cap)
    one_ids, served = lax.optimization_barrier((neigh_one_ids[0], served))
    one_high, one_low = halves(one_ids)
    one_low = jnp.where(slots < count_one, one_low, -1.0)
    one_counts = count_matrix(one_high, one_low, front, 2 * cap)
    inv_one = (1.0 / count_one.astype(F32)).reshape(feats, -1)
    frontier = swap(served, "graph")
    frontier, early = lax.optimization_barrier((frontier, early))
    rows_one = hop(frontier, one_counts, self_one_ids[0], inv_one, feats)
    rows_one, early = lax.optimization_barrier((rows_one, early))
    mine = swap(rows_one, "feat")

    weights = early[:, : 2 * width].reshape(feats * 2 * width, hidden_width)
    sent = early[:, 2 * width :].reshape(feats, -1).astype(F32)
    got = []
    start = 0
    for size in field_sizes:
        got.append(sent[:, start : start + size])
        start += size
    self_two = (got[0] * 256.0 + got[1]).astype(jnp.int32).reshape(-1)
    counts_two = got[2].reshape(-1)
    neigh_high, neigh_low = (
        value.reshape(feats, fan, share).transpose(1, 0, 2).reshape(fan, -1) for value in got[3:5]
    )
    pairs = (got[5] * 256.0 + got[6]).astype(jnp.int32).reshape(feats, 2, pair_share)
    pairs = pairs.transpose(1, 0, 2).reshape(2, -1)
    targets_total = self_two.shape[0]
    pair_total = pairs.shape[1]
    pick_neigh = count_matrix(neigh_high, neigh_low, nodes, nodes)[0]
    pick_self = one_hot(self_two, nodes)
    pick_ends = one_hot(jnp.concatenate([pairs[0], pairs[1], neg_ids[0]]), targets_total)
    pick_self, pick_ends = lax.optimization_barrier(
        (pick_self, pick_ends)
    )

    hidden_pre = dot(mine.reshape(feats * 2 * width, -1), weights, ((0,), (0,)))
    hidden = gather_all(jnp.maximum(hidden_pre, 0.0).astype(BF), "feat")
    hidden = hidden.reshape(nodes, hidden_width)

    inv_two = (1.0 / counts_two)[:, None]
    hidden_self = dot(pick_self, hidden, ((1,), (0,))).astype(BF)
    hidden_neigh = (dot(pick_neigh, hidden, ((1,), (0,))) * inv_two).astype(BF)
    embed = (
        dot(hidden_self, second_self, ((1,), (0,)))
        + dot(hidden_neigh, second_neigh, ((1,), (0,)))
    ).astype(BF)

    end_rows = dot(pick_ends, embed, ((1,), (0,))).astype(BF)
    source_rows = end_rows[:pair_total]
    dest_rows = end_rows[pair_total : 2 * pair_total]
    negative_rows = end_rows[2 * pair_total :]
    pos_score = (
        jnp.sum(source_rows.astype(F32) * dest_rows.astype(F32), axis=1, keepdims=True) * scale
    )
    neg_score = dot(source_rows, negative_rows, ((1,), (1,))) * scale
    loss_part = (
        jnp.sum(jax.nn.softplus(-pos_score)) + jnp.sum(jax.nn.softplus(neg_score)) / negative_total
    )
    pos_grad = -jax.nn.sigmoid(-pos_score)
    neg_grad = (jax.nn.sigmoid(neg_score) / negative_total).astype(BF)
    source_grad = (
        pos_grad * dest_rows.astype(F32) + dot(neg_grad, negative_rows, ((1,), (0,)))
    ) * scale
    dest_grad = pos_grad * source_rows.astype(F32) * scale
    negative_grad = dot(neg_grad, source_rows, ((0,), (0,))) * scale
    end_grads = jnp.concatenate([source_grad, dest_grad, negative_grad]).astype(BF)
    embed_grad = dot(pick_ends, end_grads, ((0,), (0,))).astype(BF)

    grad_ss = dot(hidden_self, embed_grad, ((0,), (0,)))
    grad_sn = dot(hidden_neigh, embed_grad, ((0,), (0,)))
    self_back = dot(embed_grad, second_self, ((1,), (1,))).astype(BF)
    neigh_back = (dot(embed_grad, second_neigh, ((1,), (1,))) * inv_two).astype(BF)
    hidden_grad = dot(self_back, pick_self, ((0,), (0,))) + dot(
        neigh_back, pick_neigh, ((0,), (0,))
    )
    pre_grad = jnp.where(hidden.T > 0, hidden_grad, 0.0).astype(BF)
    first_part = dot(
        rows_one.transpose(1, 0, 2).reshape(2 * width, nodes), pre_grad, ((1,), (1,))
    )

    loss_high = loss_part.astype(BF)
    loss_mid = (loss_part - loss_high.astype(F32)).astype(BF)
    loss_low = (loss_part - loss_high.astype(F32) - loss_mid.astype(F32)).astype(BF)
    lanes = lax.broadcasted_iota(jnp.int32, (graphs, 1, hidden_width), 2)
    loss_row = jnp.where(lanes == 1, loss_mid, jnp.where(lanes == 2, loss_low, loss_high))
    parts = jnp.concatenate(
        [
            first_part.astype(BF).reshape(graphs, -1, hidden_width),
            grad_ss.astype(BF).reshape(graphs, -1, hidden_width),
            grad_sn.astype(BF).reshape(graphs, -1, hidden_width),
            loss_row,
        ],
        axis=1,
    )
    sums = jnp.sum(swap(parts, "graph").astype(F32), axis=0)
    loss = jnp.sum(sums[-1, 0:3])
    first_rows = 2 * width // graphs
    second_rows = hidden_width // graphs
    whole = gather_all(sums[:-1].astype(BF), "graph").astype(F32)
    first_sums = whole[:, :first_rows].reshape(2 * width, hidden_width)
    ss = whole[:, first_rows : first_rows + second_rows].reshape(hidden_width, hidden_width)
    sn = whole[:, first_rows + second_rows :].reshape(hidden_width, hidden_width)
    return (
        first_sums[:width],
        first_sums[width:],
        ss,
        sn,
        loss / (pair_total * graphs),
    )


def solution(mesh):
    placed = (
        P("graph", "feat"),
        P("graph", None, None),
        P("graph", None),
        P("graph", None, None),
        P("graph", None),
        P("graph", "feat"),
        P("graph", None, "feat"),
        P("graph", "feat"),
        P("graph", None, "feat"),
        P("graph", None),
        P("feat", None),
        P("feat", None),
        P(),
        P(),
    )
    return jax.shard_map(
        local,
        mesh=mesh,
        in_specs=placed,
        out_specs=(P("feat", None), P("feat", None), P(), P(), P()),
        check_vma=False,
    )
```

```python
import functools
import math

import jax
import jax.numpy as jnp
from jax import lax
from jax.experimental import pallas as pl
from jax.experimental.pallas import tpu as pltpu
from jax.sharding import PartitionSpec as P

BF = jnp.bfloat16
F32 = jnp.float32
F8 = jnp.float8_e4m3fn
VMEM_LIMIT = 50 * 2**20
NN = ((1,), (0,))
NT = ((1,), (1,))
TN = ((0,), (0,))


def swap(value, axis):
    return lax.all_to_all(value, axis, split_axis=0, concat_axis=0, tiled=True)


def gather_all(value, axis):
    size = lax.axis_size(axis)
    return swap(jnp.broadcast_to(value[None], (size,) + value.shape), axis)


def dot(former, latter, dims):
    return lax.dot_general(former, latter, (dims, ((), ())), preferred_element_type=F32)


def serve_kernel(ids_ref, feat_ref, out_ref, table, picked):
    width, rows = feat_ref.shape
    groups, _, cap = out_ref.shape
    step = 512

    def fill(at, _):
        at = pl.multiple_of(at * step, step)
        table[pl.ds(at, step), 0:width] = feat_ref[:, pl.ds(at, step)].astype(F32).T
        return 0

    lax.fori_loop(0, rows // step, fill, 0)

    def per_group(group, _):
        base = group * cap

        def pick(at, _):
            for lane in range(32):
                row = at * 32 + lane
                picked[pl.ds(row, 1), :] = table[pl.ds(ids_ref[base + row], 1), :]
            return 0

        lax.fori_loop(0, cap // 32, pick, 0)
        out_ref[group] = picked[:, 0:width].T.astype(out_ref.dtype)
        return 0

    lax.fori_loop(0, groups, per_group, 0)


def serve(features_t, ids, groups, cap):
    width, rows = features_t.shape
    return pl.pallas_call(
        serve_kernel,
        out_shape=jax.ShapeDtypeStruct((groups, width, cap), features_t.dtype),
        in_specs=[
            pl.BlockSpec(memory_space=pltpu.SMEM),
            pl.BlockSpec(memory_space=pltpu.VMEM),
        ],
        out_specs=pl.BlockSpec(memory_space=pltpu.VMEM),
        scratch_shapes=[pltpu.VMEM((rows, 128), F32), pltpu.VMEM((cap, 128), F32)],
        compiler_params=pltpu.CompilerParams(vmem_limit_bytes=VMEM_LIMIT),
        name="serve",
    )(ids, features_t)


def count_kernel(keys_ref, lows_ref, out_ref, marks):
    chunks, _, chunk = out_ref.shape
    spans = chunks * chunk // 256
    across = chunk // 256

    @pl.when(pl.program_id(0) == 0)
    def _():
        marks[...] = lax.broadcasted_iota(jnp.int32, (256, 256), 0).astype(F32).astype(BF)

    def stretch(row, rows):
        small = jnp.broadcast_to(row, (16, 256)).astype(BF)
        return jnp.concatenate([small] * (rows // 16), axis=0)

    def block(pair, _):
        one = jnp.ones((256, 256), BF)
        zero = jnp.zeros((256, 256), BF)
        place = pl.multiple_of(pair * 32, 32)
        rights = []
        for at in (pair * 2, pair * 2 + 1):
            low = stretch(lows_ref[pl.ds(at, 1), :], 256)
            rights.append(jnp.where(low == marks[...], one, zero))
        for first in range(0, spans, 16):
            size = min(16, spans - first)
            parts = []
            for side in range(2):
                row = keys_ref[pl.ds(pair * 2 + side, 1), :]
                key = stretch(row - float(first * 16), size * 16)
                left = jnp.where(
                    key == marks[0 : size * 16, :], one[: size * 16], zero[: size * 16]
                )
                parts.append(dot(left, rights[side], NT))
            for inner in range(size):
                span = first + inner
                lane = (span % across) * 256
                rows = [part[inner * 16 : (inner + 1) * 16] for part in parts]
                out_ref[span // across, pl.ds(place, 32), lane : lane + 256] = jnp.concatenate(
                    rows, axis=0
                ).astype(out_ref.dtype)
        return 0

    lax.fori_loop(0, 8, block, 0, unroll=4)


def count_matrix(highs, lows, total, chunk, kind):
    fan, nodes = highs.shape

    def order(value):
        return value.reshape(fan, nodes // 16, 16).transpose(1, 0, 2).reshape(nodes // 16, -1)

    node = (lax.broadcasted_iota(jnp.int32, (fan, nodes), 1) % 16).astype(F32)
    keys = order(highs * 16.0 + node)
    return pl.pallas_call(
        count_kernel,
        grid=(nodes // 256,),
        out_shape=jax.ShapeDtypeStruct((total // chunk, nodes, chunk), kind),
        in_specs=[
            pl.BlockSpec((16, 256), lambda at: (at, 0)),
            pl.BlockSpec((16, 256), lambda at: (at, 0)),
        ],
        out_specs=pl.BlockSpec((total // chunk, 256, chunk), lambda at: (0, at, 0)),
        scratch_shapes=[pltpu.VMEM((256, 256), BF)],
        compiler_params=pltpu.CompilerParams(vmem_limit_bytes=VMEM_LIMIT),
        cost_estimate=pl.CostEstimate(
            flops=2 * nodes * total * 256,
            bytes_accessed=2 * nodes * total,
            transcendentals=0,
        ),
        name="count_matrix",
    )(keys, order(lows))


def hop_kernel(self_ref, counts_ref, front_ref, inv_ref, out_ref, table, total, own):
    owners, width, cap = front_ref.shape
    blocks, _, block = out_ref.shape
    step = pl.program_id(0)
    parts = []
    for owner in range(owners):
        rows = front_ref[owner].astype(F32).T
        at = pl.multiple_of((step * owners + owner) * cap, cap)
        table[pl.ds(at, cap), 0:width] = rows
        parts.append(rows.astype(BF))
    part = dot(counts_ref[0].astype(BF), jnp.concatenate(parts, axis=0), NN)

    @pl.when(step == 0)
    def _():
        total[...] = part

    @pl.when(step > 0)
    def _():
        total[...] += part

    @pl.when(step == pl.num_programs(0) - 1)
    def _():
        def per_block(dest, _):
            base = pl.multiple_of(dest * block, block)

            def pick(at, _):
                for lane in range(32):
                    row = at * 32 + lane
                    own[pl.ds(row, 1), :] = table[pl.ds(self_ref[base + row], 1), :]
                return 0

            lax.fori_loop(0, block // 32, pick, 0)
            out_ref[dest, 0:width, :] = own[:, 0:width].T.astype(BF)
            mean = total[pl.ds(base, block), :].T * inv_ref[pl.ds(dest, 1), :]
            out_ref[dest, width : 2 * width, :] = mean.astype(BF)
            return 0

        lax.fori_loop(0, blocks, per_block, 0)


def hop(frontier, counts, self_ids, inv, blocks):
    owners, width, cap = frontier.shape
    chunks, nodes, chunk = counts.shape
    block = nodes // blocks
    per = chunk // cap
    return pl.pallas_call(
        hop_kernel,
        grid=(chunks,),
        out_shape=jax.ShapeDtypeStruct((blocks, 2 * width, block), BF),
        in_specs=[
            pl.BlockSpec(memory_space=pltpu.SMEM),
            pl.BlockSpec((1, nodes, chunk), lambda at: (at, 0, 0)),
            pl.BlockSpec((per, width, cap), lambda at: (at, 0, 0)),
            pl.BlockSpec(inv.shape, lambda at: (0, 0)),
        ],
        out_specs=pl.BlockSpec((blocks, 2 * width, block), lambda at: (0, 0, 0)),
        scratch_shapes=[
            pltpu.VMEM((owners * cap, 128), F32),
            pltpu.VMEM((nodes, width), F32),
            pltpu.VMEM((block, 128), F32),
        ],
        compiler_params=pltpu.CompilerParams(vmem_limit_bytes=VMEM_LIMIT),
        cost_estimate=pl.CostEstimate(
            flops=2 * nodes * chunks * chunk * 128,
            bytes_accessed=nodes * chunks * chunk,
            transcendentals=0,
        ),
        name="first_hop",
    )(self_ids, counts, frontier, inv)


def mark_rows(ids_ref, out_ref, marks):
    total, count = out_ref.shape
    one = jnp.ones((256, count), BF); zero = jnp.zeros((256, count), BF)
    for first in range(0, total, 256):
        row = jnp.broadcast_to(ids_ref[...] - float(first), (16, count)).astype(BF)
        row = jnp.concatenate([row] * 16, axis=0)
        out_ref[first:first + 256, :] = jnp.where(row == marks, one, zero)

def second_kernel(scale, negative_total, hidden_ref, rows_ref, self_ref, ends_ref, inv_ref, ws_ref, wn_ref, neigh_hbm,
                  first_ref, second_ref, loss_ref, neigh, own, ends, hidden_t, sem):
    copy = pltpu.make_async_copy(neigh_hbm, neigh, sem)
    copy.start()
    blocks, width, block = hidden_ref.shape
    for at in range(blocks):
        hidden_t[:, at * block:(at + 1) * block] = hidden_ref[at]
    targets = own.shape[1]
    marks = lax.broadcasted_iota(jnp.int32, (256, targets), 0).astype(F32).astype(BF)
    mark_rows(self_ref, own, marks)
    mark_rows(ends_ref, ends, marks)
    inv = inv_ref[...]
    hidden = hidden_t[...]
    hs = dot(hidden, own[...], NN).astype(BF)
    copy.wait()
    hn = (dot(hidden, neigh[...], NT) * inv).astype(BF)
    embed = (dot(ws_ref[...], hs, TN) + dot(wn_ref[...], hn, TN)).astype(BF)
    rows = dot(embed, ends[...], NN).astype(BF)
    count = rows.shape[1] // 3
    source, dest, negative = rows[:, :count], rows[:, count:2 * count], rows[:, 2 * count:]
    pos = jnp.sum(source.astype(F32) * dest.astype(F32), axis=0, keepdims=True) * scale
    neg = dot(source, negative, TN) * scale
    small = jnp.exp(-jnp.abs(neg))
    neg_sig = jnp.where(neg >= 0, 1.0, small) / (1.0 + small)
    neg_loss = jnp.maximum(neg, 0.0) + jnp.log1p(small)
    small = jnp.exp(-jnp.abs(pos))
    pos_grad = -(jnp.where(pos >= 0, small, 1.0) / (1.0 + small))
    pos_loss = jnp.maximum(-pos, 0.0) + jnp.log1p(small)
    loss = jnp.sum(neg_loss, axis=0, keepdims=True) * (1.0 / negative_total) + pos_loss
    loss_ref[...] = jnp.broadcast_to(jnp.sum(loss, axis=1, keepdims=True), loss_ref.shape)
    neg_grad = (neg_sig * (1.0 / negative_total)).astype(BF)
    source_grad = (pos_grad * dest.astype(F32) + dot(negative, neg_grad, NT)) * scale
    dest_grad = pos_grad * source.astype(F32) * scale
    negative_grad = dot(source, neg_grad, NN) * scale
    grads = jnp.concatenate([source_grad.astype(BF), dest_grad.astype(BF), negative_grad.astype(BF)], axis=1)
    eg = dot(grads, ends[...], NT).astype(BF)
    width2 = ws_ref.shape[0]
    second_ref[0:width2, :] = dot(hs, eg, NT).astype(BF)
    second_ref[width2:2 * width2, :] = dot(hn, eg, NT).astype(BF)
    self_back = dot(ws_ref[...], eg, NN).astype(BF)
    neigh_back = (dot(wn_ref[...], eg, NN) * inv).astype(BF)
    hidden_grad = dot(self_back, own[...], NT) + dot(neigh_back, neigh[...], NN)
    pre = jnp.where(hidden > 0, hidden_grad, 0.0).astype(BF)
    rows_one = jnp.concatenate([rows_ref[at] for at in range(blocks)], axis=1)
    first_ref[...] = dot(rows_one, pre, NT).astype(BF)

def second(hidden, rows_one, pick_neigh, self_two, ends, inv, ws, wn, scale, negative_total):
    blocks, width, block = hidden.shape
    nodes = blocks * block
    targets = self_two.shape[1]
    many = ends.shape[1]
    vm = pl.BlockSpec(memory_space=pltpu.VMEM)
    return pl.pallas_call(functools.partial(second_kernel, scale, negative_total),
        out_shape=[jax.ShapeDtypeStruct((rows_one.shape[1], width), BF), jax.ShapeDtypeStruct((2 * width, width), BF), jax.ShapeDtypeStruct((8, width), F32)],
        in_specs=[vm] * 7 + [pl.BlockSpec(memory_space=pl.ANY)],
        out_specs=[vm] * 3,
        scratch_shapes=[pltpu.VMEM((targets, nodes), BF), pltpu.VMEM((nodes, targets), BF), pltpu.VMEM((targets, many), BF), pltpu.VMEM((width, nodes), BF), pltpu.SemaphoreType.DMA],
        compiler_params=pltpu.CompilerParams(vmem_limit_bytes=VMEM_LIMIT),
        name="second_layer")(hidden, rows_one, self_two, ends, inv, ws, wn, pick_neigh)

def halves(ids):
    return (ids // 256).astype(F32), (ids % 256).astype(F32)


def local(
    features,
    frontier_ids,
    self_one_ids,
    neigh_one_ids,
    count_one,
    self_two_ids,
    neigh_two_ids,
    count_two,
    pos_pairs,
    neg_ids,
    first_self,
    first_neigh,
    second_self,
    second_neigh,
):
    graphs = lax.axis_size("graph")
    feats = lax.axis_size("feat")
    hidden_width = second_self.shape[0]
    scale = 1.0 / math.sqrt(hidden_width)
    negative_total = neg_ids.shape[1]
    nodes = self_one_ids.shape[1]
    fan = neigh_one_ids.shape[1]
    width = features.shape[1]
    cap = frontier_ids.shape[2]
    front = graphs * cap
    share = self_two_ids.shape[1]
    pair_share = pos_pairs.shape[2]

    asked = swap(frontier_ids[0], "graph")

    slots = lax.broadcasted_iota(jnp.int32, (fan, 1), 0)
    neigh_high, neigh_low = halves(neigh_two_ids[0])
    neigh_low = jnp.where(slots < count_two, neigh_low, -1.0)
    fields = [*halves(self_two_ids), count_two.astype(F32), neigh_high, neigh_low]
    fields = [field.reshape(-1) for field in fields + list(halves(pos_pairs[0]))]
    field_sizes = [field.shape[0] for field in fields]
    spare = (128 - 2 * width) * hidden_width - sum(field_sizes)
    fields = jnp.concatenate(fields + [jnp.zeros((spare,), F32)]).astype(BF)
    early = jnp.concatenate(
        [first_self, first_neigh, fields.reshape(-1, hidden_width)], axis=0
    )
    early = lax.all_gather(early, "feat")

    served = serve(features.T, asked.reshape(-1), graphs, cap)
    one_ids, served = lax.optimization_barrier((neigh_one_ids[0], served))
    one_high, one_low = halves(one_ids)
    one_low = jnp.where(slots < count_one, one_low, -1.0)
    one_counts = count_matrix(one_high, one_low, front, 2 * cap, F8)
    inv_one = (1.0 / count_one.astype(F32)).reshape(feats, -1)
    frontier = swap(served, "graph")
    frontier, early = lax.optimization_barrier((frontier, early))
    rows_one = hop(frontier, one_counts, self_one_ids[0], inv_one, feats)
    rows_one, early = lax.optimization_barrier((rows_one, early))
    mine = swap(rows_one, "feat")

    weights = early[:, : 2 * width].reshape(feats * 2 * width, hidden_width)
    sent = early[:, 2 * width :].reshape(feats, -1).astype(F32)
    got = []
    start = 0
    for size in field_sizes:
        got.append(sent[:, start : start + size])
        start += size
    self_two = (got[0] * 256.0 + got[1]).reshape(1, -1)
    inv_two = 1.0 / got[2].reshape(1, -1)
    neigh_high, neigh_low = (
        value.reshape(feats, fan, share).transpose(1, 0, 2).reshape(fan, -1) for value in got[3:5]
    )
    pairs = (got[5] * 256.0 + got[6]).reshape(feats, 2, pair_share).transpose(1, 0, 2)
    pair_total = feats * pair_share
    ends = jnp.concatenate([pairs.reshape(1, -1), neg_ids.astype(F32)], axis=1)
    pick_neigh = count_matrix(neigh_high, neigh_low, nodes, nodes, BF)[0]

    hidden_pre = dot(weights, mine.reshape(feats * 2 * width, -1), TN)
    hidden = gather_all(jnp.maximum(hidden_pre, 0.0).astype(BF), "feat")
    first_part, second_part, loss_part = second(
        hidden,
        rows_one,
        pick_neigh,
        self_two,
        ends,
        inv_two,
        second_self,
        second_neigh,
        scale,
        negative_total,
    )
    loss_part = loss_part[0, 0]

    loss_high = loss_part.astype(BF)
    loss_mid = (loss_part - loss_high.astype(F32)).astype(BF)
    loss_low = (loss_part - loss_high.astype(F32) - loss_mid.astype(F32)).astype(BF)
    lanes = lax.broadcasted_iota(jnp.int32, (graphs, 1, hidden_width), 2)
    loss_row = jnp.where(lanes == 1, loss_mid, jnp.where(lanes == 2, loss_low, loss_high))
    parts = jnp.concatenate(
        [
            first_part.reshape(graphs, -1, hidden_width),
            second_part.reshape(graphs, -1, hidden_width),
            loss_row,
        ],
        axis=1,
    )
    sums = jnp.sum(swap(parts, "graph").astype(F32), axis=0)
    loss = jnp.sum(sums[-1, 0:3])
    first_rows = 2 * width // graphs
    whole = gather_all(sums[:-1].astype(BF), "graph").astype(F32)
    first_sums = whole[:, :first_rows].reshape(2 * width, hidden_width)
    second_sums = whole[:, first_rows:].reshape(2 * hidden_width, hidden_width)
    return (
        first_sums[:width],
        first_sums[width:],
        second_sums[:hidden_width],
        second_sums[hidden_width:],
        loss / (pair_total * graphs),
    )


def solution(mesh):
    placed = (
        P("graph", "feat"),
        P("graph", None, None),
        P("graph", None),
        P("graph", None, None),
        P("graph", None),
        P("graph", "feat"),
        P("graph", None, "feat"),
        P("graph", "feat"),
        P("graph", None, "feat"),
        P("graph", None),
        P("feat", None),
        P("feat", None),
        P(),
        P(),
    )
    return jax.shard_map(
        local,
        mesh=mesh,
        in_specs=placed,
        out_specs=(P("feat", None), P("feat", None), P(), P(), P()),
        check_vma=False,
    )
```

```python
import functools
import math

import jax
import jax.numpy as jnp
from jax import lax
from jax.experimental import pallas as pl
from jax.experimental.pallas import tpu as pltpu
from jax.sharding import PartitionSpec as P

BF = jnp.bfloat16
F32 = jnp.float32
F8 = jnp.float8_e4m3fn
VMEM_LIMIT = 50 * 2**20
NN = ((1,), (0,))
NT = ((1,), (1,))
TN = ((0,), (0,))


def swap(value, axis):
    return lax.all_to_all(value, axis, split_axis=0, concat_axis=0, tiled=True)


def gather_all(value, axis):
    size = lax.axis_size(axis)
    return swap(jnp.broadcast_to(value[None], (size,) + value.shape), axis)


def dot(former, latter, dims):
    return lax.dot_general(former, latter, (dims, ((), ())), preferred_element_type=F32)


def serve_kernel(ids_ref, feat_ref, out_ref, table, picked):
    width, rows = feat_ref.shape
    groups, _, cap = out_ref.shape
    step = 512

    def fill(at, _):
        at = pl.multiple_of(at * step, step)
        table[pl.ds(at, step), 0:width] = feat_ref[:, pl.ds(at, step)].astype(F32).T
        return 0

    lax.fori_loop(0, rows // step, fill, 0)

    def take(group, side):
        for row in range(cap):
            picked[side, row : row + 1, :] = table[pl.ds(ids_ref[group * cap + row], 1), :]

    def put(group, side):
        out_ref[group] = picked[side, :, 0:width].T.astype(out_ref.dtype)

    def two(at, _):
        group = at * 2 + 1
        take(group, 1)
        put(group - 1, 0)
        take(group + 1, 0)
        put(group, 1)
        return 0

    take(0, 0)
    lax.fori_loop(0, groups // 2 - 1, two, 0)
    take(groups - 1, 1)
    put(groups - 2, 0)
    put(groups - 1, 1)


def serve(features_t, ids, groups, cap):
    width, rows = features_t.shape
    return pl.pallas_call(
        serve_kernel,
        out_shape=jax.ShapeDtypeStruct((groups, width, cap), features_t.dtype),
        in_specs=[
            pl.BlockSpec(memory_space=pltpu.SMEM),
            pl.BlockSpec(memory_space=pltpu.VMEM),
        ],
        out_specs=pl.BlockSpec(memory_space=pltpu.VMEM),
        scratch_shapes=[pltpu.VMEM((rows, 128), F32), pltpu.VMEM((2, cap, 128), F32)],
        compiler_params=pltpu.CompilerParams(vmem_limit_bytes=VMEM_LIMIT),
        name="serve",
    )(ids, features_t)


def count_kernel(keys_ref, lows_ref, out_ref, marks):
    chunks, _, chunk = out_ref.shape
    spans = chunks * chunk // 256
    across = chunk // 256

    @pl.when(pl.program_id(0) == 0)
    def _():
        marks[...] = lax.broadcasted_iota(jnp.int32, (256, 256), 0).astype(F32).astype(BF)

    def stretch(row, rows):
        small = jnp.broadcast_to(row, (16, 256)).astype(BF)
        return jnp.concatenate([small] * (rows // 16), axis=0)

    def block(pair, _):
        one = jnp.ones((256, 256), BF)
        zero = jnp.zeros((256, 256), BF)
        place = pl.multiple_of(pair * 32, 32)
        rights = []
        for at in (pair * 2, pair * 2 + 1):
            low = stretch(lows_ref[pl.ds(at, 1), :], 256)
            rights.append(jnp.where(low == marks[...], one, zero))
        for first in range(0, spans, 16):
            size = min(16, spans - first)
            parts = []
            for side in range(2):
                row = keys_ref[pl.ds(pair * 2 + side, 1), :]
                key = stretch(row - float(first * 16), size * 16)
                left = jnp.where(
                    key == marks[0 : size * 16, :], one[: size * 16], zero[: size * 16]
                )
                parts.append(dot(left, rights[side], NT))
            for inner in range(size):
                span = first + inner
                lane = (span % across) * 256
                rows = [part[inner * 16 : (inner + 1) * 16] for part in parts]
                out_ref[span // across, pl.ds(place, 32), lane : lane + 256] = jnp.concatenate(
                    rows, axis=0
                ).astype(out_ref.dtype)
        return 0

    lax.fori_loop(0, 8, block, 0, unroll=4)


def count_matrix(highs, lows, total, chunk, kind):
    fan, nodes = highs.shape

    def order(value):
        return value.reshape(fan, nodes // 16, 16).transpose(1, 0, 2).reshape(nodes // 16, -1)

    node = (lax.broadcasted_iota(jnp.int32, (fan, nodes), 1) % 16).astype(F32)
    keys = order(highs * 16.0 + node)
    return pl.pallas_call(
        count_kernel,
        grid=(nodes // 256,),
        out_shape=jax.ShapeDtypeStruct((total // chunk, nodes, chunk), kind),
        in_specs=[
            pl.BlockSpec((16, 256), lambda at: (at, 0)),
            pl.BlockSpec((16, 256), lambda at: (at, 0)),
        ],
        out_specs=pl.BlockSpec((total // chunk, 256, chunk), lambda at: (0, at, 0)),
        scratch_shapes=[pltpu.VMEM((256, 256), BF)],
        compiler_params=pltpu.CompilerParams(vmem_limit_bytes=VMEM_LIMIT),
        cost_estimate=pl.CostEstimate(
            flops=2 * nodes * total * 256,
            bytes_accessed=2 * nodes * total,
            transcendentals=0,
        ),
        name="count_matrix",
    )(keys, order(lows))


def hop_kernel(
    steps, self_ref, counts_ref, front_ref, inv_ref, out_ref, table, total, own, up, down
):
    owners, width, cap = front_ref.shape
    blocks, _, block = out_ref.shape
    step = pl.program_id(0)
    per = owners // steps
    half = steps // 2

    @pl.when(step == 0)
    def _():
        most = jnp.abs(front_ref[0])
        for owner in range(1, owners):
            most = jnp.maximum(most, jnp.abs(front_ref[owner]))
        most = jnp.max(most.astype(F32), axis=1, keepdims=True)
        power = jnp.ones_like(most)
        back = jnp.ones_like(most)
        for exponent in (32, 32, 16, 16, 8, 4, 2, 1):
            fits = most * power * 2.0**exponent <= 224.0
            power = jnp.where(fits, power * 2.0**exponent, power)
            back = jnp.where(fits, back * 2.0**-exponent, back)
        up[...] = jnp.broadcast_to(power, up.shape)
        down[...] = jnp.broadcast_to(back, down.shape)
        total[...] = jnp.zeros_like(total)

    def product():
        front = jnp.concatenate([front_ref[step * per + at] for at in range(per)], axis=1)
        front = front.astype(F32) * up[:, 0:1]
        high = front.astype(F8)
        low = ((front - high.astype(F32)) * 16.0).astype(F8)
        part = dot(jnp.concatenate([high, low], axis=0), counts_ref[0], NT)
        total[...] += part[:width] + part[width:] * (1.0 / 16.0)

    @pl.when(step < half)
    def _():
        for at in range(owners // half):
            owner = step * (owners // half) + at
            place = pl.multiple_of(owner * cap, cap)
            table[pl.ds(place, cap), 0:width] = front_ref[owner].astype(F32).T
        product()

    @pl.when(step >= half)
    def _():
        for at in range(blocks // half):
            dest = (step - half) * (blocks // half) + at
            for row in range(block):
                place = at * block + row
                own[place : place + 1, :] = table[pl.ds(self_ref[dest * block + row], 1), :]
            rows = own[at * block : (at + 1) * block, 0:width]
            out_ref[dest, 0:width, :] = rows.T.astype(BF)
        product()

    @pl.when(step == steps - 1)
    def _():
        back = down[:, 0:1]
        for dest in range(blocks):
            mean = total[:, dest * block : (dest + 1) * block] * back
            out_ref[dest, width : 2 * width, :] = (mean * inv_ref[dest : dest + 1, :]).astype(BF)


def hop(frontier, counts, self_ids, inv, blocks):
    owners, width, cap = frontier.shape
    chunks, nodes, chunk = counts.shape
    block = nodes // blocks
    return pl.pallas_call(
        functools.partial(hop_kernel, chunks),
        grid=(chunks,),
        out_shape=jax.ShapeDtypeStruct((blocks, 2 * width, block), BF),
        in_specs=[
            pl.BlockSpec(memory_space=pltpu.SMEM),
            pl.BlockSpec((1, nodes, chunk), lambda at: (at, 0, 0)),
            pl.BlockSpec((owners, width, cap), lambda at: (0, 0, 0)),
            pl.BlockSpec(inv.shape, lambda at: (0, 0)),
        ],
        out_specs=pl.BlockSpec((blocks, 2 * width, block), lambda at: (0, 0, 0)),
        scratch_shapes=[
            pltpu.VMEM((owners * cap, 128), F32),
            pltpu.VMEM((width, nodes), F32),
            pltpu.VMEM((nodes * 2 // chunks, 128), F32),
            pltpu.VMEM((width, 128), F32),
            pltpu.VMEM((width, 128), F32),
        ],
        compiler_params=pltpu.CompilerParams(vmem_limit_bytes=VMEM_LIMIT),
        cost_estimate=pl.CostEstimate(
            flops=2 * nodes * chunks * chunk * 128,
            bytes_accessed=nodes * chunks * chunk,
            transcendentals=0,
        ),
        name="first_hop",
    )(self_ids, counts, frontier, inv)


def first_kernel(mine_ref, early_ref, out_ref):
    feats, depth, block = mine_ref.shape
    weights = early_ref[:, 0:depth, :].reshape(feats * depth, early_ref.shape[2])
    pre = dot(weights, mine_ref[...].reshape(feats * depth, block), TN)
    hidden = jnp.maximum(pre, 0.0).astype(BF)
    for at in range(out_ref.shape[0]):
        out_ref[at] = hidden


def first(mine, early):
    feats, _, block = mine.shape
    return pl.pallas_call(
        first_kernel,
        out_shape=jax.ShapeDtypeStruct((feats, early.shape[2], block), BF),
        compiler_params=pltpu.CompilerParams(vmem_limit_bytes=VMEM_LIMIT),
        name="first_layer",
    )(mine, early)


def mark_rows(ids_ref, out_ref, marks):
    total, count = out_ref.shape
    one = jnp.ones((256, count), BF); zero = jnp.zeros((256, count), BF)
    for first in range(0, total, 256):
        row = jnp.broadcast_to(ids_ref[...] - float(first), (16, count)).astype(BF)
        row = jnp.concatenate([row] * 16, axis=0)
        out_ref[first:first + 256, :] = jnp.where(row == marks, one, zero)

def second_kernel(scale, negative_total, hidden_ref, rows_ref, self_ref, ends_ref, inv_ref, ws_ref, wn_ref, neigh_hbm,
                  out_ref, neigh, own, ends, hidden_t, sem):
    copy = pltpu.make_async_copy(neigh_hbm, neigh, sem)
    copy.start()
    blocks, width, block = hidden_ref.shape
    for at in range(blocks):
        hidden_t[:, at * block:(at + 1) * block] = hidden_ref[at]
    targets = own.shape[1]
    marks = lax.broadcasted_iota(jnp.int32, (256, targets), 0).astype(F32).astype(BF)
    mark_rows(self_ref, own, marks)
    mark_rows(ends_ref, ends, marks)
    inv = inv_ref[...]
    hidden = hidden_t[...]
    hs = dot(hidden, own[...], NN).astype(BF)
    copy.wait()
    hn = (dot(hidden, neigh[...], NT) * inv).astype(BF)
    embed = (dot(ws_ref[...], hs, TN) + dot(wn_ref[...], hn, TN)).astype(BF)
    rows = dot(embed, ends[...], NN).astype(BF)
    count = rows.shape[1] // 3
    source, dest, negative = rows[:, :count], rows[:, count:2 * count], rows[:, 2 * count:]
    pos = jnp.sum(source.astype(F32) * dest.astype(F32), axis=0, keepdims=True) * scale
    neg = dot(source, negative, TN) * scale
    small = jnp.exp(-jnp.abs(neg))
    neg_sig = jnp.where(neg >= 0, 1.0, small) / (1.0 + small)
    neg_loss = jnp.maximum(neg, 0.0) + jnp.log1p(small)
    small = jnp.exp(-jnp.abs(pos))
    pos_grad = -(jnp.where(pos >= 0, small, 1.0) / (1.0 + small))
    pos_loss = jnp.maximum(-pos, 0.0) + jnp.log1p(small)
    loss = jnp.sum(neg_loss, axis=0, keepdims=True) * (1.0 / negative_total) + pos_loss
    loss = jnp.sum(loss, axis=1, keepdims=True)
    neg_grad = (neg_sig * (1.0 / negative_total)).astype(BF)
    source_grad = (pos_grad * dest.astype(F32) + dot(negative, neg_grad, NT)) * scale
    dest_grad = pos_grad * source.astype(F32) * scale
    negative_grad = dot(source, neg_grad, NN) * scale
    grads = jnp.concatenate([source_grad.astype(BF), dest_grad.astype(BF), negative_grad.astype(BF)], axis=1)
    eg = dot(grads, ends[...], NT).astype(BF)
    groups = out_ref.shape[0]
    many = 2 * ws_ref.shape[0] // groups
    sums = jnp.concatenate([dot(hs, eg, NT), dot(hn, eg, NT)], axis=0).astype(BF)
    for group in range(groups):
        out_ref[group, 0:many, :] = sums[group * many : (group + 1) * many]
    self_back = dot(ws_ref[...], eg, NN).astype(BF)
    neigh_back = (dot(wn_ref[...], eg, NN) * inv).astype(BF)
    hidden_grad = dot(self_back, own[...], NT) + dot(neigh_back, neigh[...], NN)
    pre = jnp.where(hidden > 0, hidden_grad, 0.0).astype(BF)
    rows_one = jnp.concatenate([rows_ref[at] for at in range(blocks)], axis=1)
    part = dot(rows_one, pre, NT)
    few = part.shape[0] // groups
    high = loss.astype(BF).astype(F32)
    mid = (loss - high).astype(BF).astype(F32)
    low = loss - high - mid
    lanes = lax.broadcasted_iota(jnp.int32, (8 - few, part.shape[1]), 1)
    tail = jnp.where(lanes == 0, high, jnp.where(lanes == 1, mid, low))
    for group in range(groups):
        rows = jnp.concatenate([part[group * few : (group + 1) * few], tail], axis=0)
        out_ref[group, many : many + 8, :] = rows.astype(BF)


def second(
    hidden, rows_one, pick_neigh, self_two, ends, inv, ws, wn, scale, negative_total, groups
):
    blocks, width, block = hidden.shape
    nodes = blocks * block
    targets = self_two.shape[1]
    many = ends.shape[1]
    vm = pl.BlockSpec(memory_space=pltpu.VMEM)
    return pl.pallas_call(functools.partial(second_kernel, scale, negative_total),
        out_shape=jax.ShapeDtypeStruct((groups, 2 * width // groups + 8, width), BF),
        in_specs=[vm] * 7 + [pl.BlockSpec(memory_space=pl.ANY)],
        out_specs=vm,
        scratch_shapes=[pltpu.VMEM((targets, nodes), BF), pltpu.VMEM((nodes, targets), BF), pltpu.VMEM((targets, many), BF), pltpu.VMEM((width, nodes), BF), pltpu.SemaphoreType.DMA],
        compiler_params=pltpu.CompilerParams(vmem_limit_bytes=VMEM_LIMIT),
        name="second_layer")(hidden, rows_one, self_two, ends, inv, ws, wn, pick_neigh)

def halves(ids):
    return (ids // 256).astype(F32), (ids % 256).astype(F32)


def local(
    features,
    frontier_ids,
    self_one_ids,
    neigh_one_ids,
    count_one,
    self_two_ids,
    neigh_two_ids,
    count_two,
    pos_pairs,
    neg_ids,
    first_self,
    first_neigh,
    second_self,
    second_neigh,
):
    graphs = lax.axis_size("graph")
    feats = lax.axis_size("feat")
    hidden_width = second_self.shape[0]
    scale = 1.0 / math.sqrt(hidden_width)
    negative_total = neg_ids.shape[1]
    nodes = self_one_ids.shape[1]
    fan = neigh_one_ids.shape[1]
    width = features.shape[1]
    cap = frontier_ids.shape[2]
    front = graphs * cap
    share = self_two_ids.shape[1]
    pair_share = pos_pairs.shape[2]

    asked = swap(frontier_ids[0], "graph")

    slots = lax.broadcasted_iota(jnp.int32, (fan, 1), 0)
    neigh_high, neigh_low = halves(neigh_two_ids[0])
    neigh_low = jnp.where(slots < count_two, neigh_low, -1.0)
    fields = [*halves(self_two_ids), count_two.astype(F32), neigh_high, neigh_low]
    fields = [field.reshape(-1) for field in fields + list(halves(pos_pairs[0]))]
    field_sizes = [field.shape[0] for field in fields]
    spare = -sum(field_sizes) % (16 * hidden_width)
    fields = jnp.concatenate(fields + [jnp.zeros((spare,), F32)]).astype(BF)
    early = jnp.concatenate(
        [first_self, first_neigh, fields.reshape(-1, hidden_width)], axis=0
    )
    early = gather_all(early, "feat")

    served = serve(features.T, asked.reshape(-1), graphs, cap)
    one_ids, served = lax.optimization_barrier((neigh_one_ids[0], served))
    one_high, one_low = halves(one_ids)
    one_low = jnp.where(slots < count_one, one_low, -1.0)
    one_counts = count_matrix(one_high, one_low, front, 2 * cap, F8)
    inv_one = (1.0 / count_one.astype(F32)).reshape(feats, -1)
    frontier = swap(served, "graph")
    frontier, early = lax.optimization_barrier((frontier, early))
    rows_one = hop(frontier, one_counts, self_one_ids[0], inv_one, feats)
    hidden = first(swap(rows_one, "feat"), early)
    hidden, early = lax.optimization_barrier((hidden, early))
    hidden = swap(hidden, "feat")

    sent = early[:, 2 * width :].reshape(feats, -1).astype(F32)
    got = []
    start = 0
    for size in field_sizes:
        got.append(sent[:, start : start + size])
        start += size
    self_two = (got[0] * 256.0 + got[1]).reshape(1, -1)
    inv_two = 1.0 / got[2].reshape(1, -1)
    neigh_high, neigh_low = (
        value.reshape(feats, fan, share).transpose(1, 0, 2).reshape(fan, -1) for value in got[3:5]
    )
    pairs = (got[5] * 256.0 + got[6]).reshape(feats, 2, pair_share).transpose(1, 0, 2)
    pair_total = feats * pair_share
    ends = jnp.concatenate([pairs.reshape(1, -1), neg_ids.astype(F32)], axis=1)
    pick_neigh = count_matrix(neigh_high, neigh_low, nodes, nodes, BF)[0]

    parts = second(
        hidden,
        rows_one,
        pick_neigh,
        self_two,
        ends,
        inv_two,
        second_self,
        second_neigh,
        scale,
        negative_total,
        graphs,
    )

    sums = jnp.sum(swap(parts, "graph").astype(F32), axis=0)
    loss = jnp.sum(sums[-1, 0:3])
    whole = gather_all(sums.astype(BF), "graph").astype(F32)
    second_rows = 2 * hidden_width // graphs
    first_rows = 2 * width // graphs
    second_sums = whole[:, :second_rows].reshape(2 * hidden_width, hidden_width)
    first_sums = whole[:, second_rows : second_rows + first_rows].reshape(-1, hidden_width)
    return (
        first_sums[:width],
        first_sums[width:],
        second_sums[:hidden_width],
        second_sums[hidden_width:],
        loss / (pair_total * graphs),
    )


def solution(mesh):
    placed = (
        P("graph", "feat"),
        P("graph", None, None),
        P("graph", None),
        P("graph", None, None),
        P("graph", None),
        P("graph", "feat"),
        P("graph", None, "feat"),
        P("graph", "feat"),
        P("graph", None, "feat"),
        P("graph", None),
        P("feat", None),
        P("feat", None),
        P(),
        P(),
    )
    return jax.shard_map(
        local,
        mesh=mesh,
        in_specs=placed,
        out_specs=(P("feat", None), P("feat", None), P(), P(), P()),
        check_vma=False,
    )
```

```python
import functools
import math

import jax
import jax.numpy as jnp
from jax import lax
from jax.experimental import pallas as pl
from jax.experimental.pallas import tpu as pltpu
from jax.sharding import PartitionSpec as P

BF = jnp.bfloat16
F32 = jnp.float32
F8 = jnp.float8_e4m3fn
VMEM_LIMIT = 50 * 2**20
NN = ((1,), (0,))
NT = ((1,), (1,))
TN = ((0,), (0,))


def swap(value, axis):
    return lax.all_to_all(value, axis, split_axis=0, concat_axis=0, tiled=True)


def gather_all(value, axis):
    size = lax.axis_size(axis)
    return swap(jnp.broadcast_to(value[None], (size,) + value.shape), axis)


def dot(former, latter, dims):
    return lax.dot_general(former, latter, (dims, ((), ())), preferred_element_type=F32)


def serve_kernel(ids_ref, feat_ref, out_ref, table, picked):
    width, rows = feat_ref.shape
    groups, _, cap = out_ref.shape
    step = 512

    def fill(at, _):
        at = pl.multiple_of(at * step, step)
        table[pl.ds(at, step), 0:width] = feat_ref[:, pl.ds(at, step)].astype(F32).T
        return 0

    lax.fori_loop(0, rows // step, fill, 0)

    def take(group, side):
        for row in range(0, cap, 8):
            rows = [
                table[pl.ds(ids_ref[group * cap + row + at], 1), :] for at in range(8)
            ]
            picked[side, row : row + 8, :] = jnp.concatenate(rows, axis=0)

    def put(group, side):
        out_ref[group] = picked[side, :, 0:width].T.astype(out_ref.dtype)

    def two(at, _):
        group = at * 2 + 1
        take(group, 1)
        put(group - 1, 0)
        take(group + 1, 0)
        put(group, 1)
        return 0

    take(0, 0)
    lax.fori_loop(0, groups // 2 - 1, two, 0)
    take(groups - 1, 1)
    put(groups - 2, 0)
    put(groups - 1, 1)


def serve(features_t, ids, groups, cap):
    width, rows = features_t.shape
    return pl.pallas_call(
        serve_kernel,
        out_shape=jax.ShapeDtypeStruct((groups, width, cap), features_t.dtype),
        in_specs=[
            pl.BlockSpec(memory_space=pltpu.SMEM),
            pl.BlockSpec(memory_space=pltpu.VMEM),
        ],
        out_specs=pl.BlockSpec(memory_space=pltpu.VMEM),
        scratch_shapes=[pltpu.VMEM((rows, 128), F32), pltpu.VMEM((2, cap, 128), F32)],
        compiler_params=pltpu.CompilerParams(vmem_limit_bytes=VMEM_LIMIT),
        name="serve",
    )(ids, features_t)


def pack_kernel(
    across, self_ref, neigh_ref, count_ref, pairs_ref, ws_ref, wn_ref, feat_ref, out_ref, copy_ref, rows
):
    copy_ref[...] = feat_ref[...]
    width = ws_ref.shape[0]
    fan, share = neigh_ref.shape
    pairs = pairs_ref.shape[1]

    def place(ids):
        return (ids & 127) * across + (ids >> 7)

    rows[...] = jnp.zeros_like(rows)
    neigh = place(neigh_ref[...])
    live = lax.broadcasted_iota(jnp.int32, (fan, share), 0) < count_ref[...]
    rows[0:fan, 0:share] = jnp.where(live, neigh & 255, -1).astype(F32)
    rows[0:fan, 128 : 128 + share] = (neigh >> 8).astype(F32)
    own = place(self_ref[...])
    rows[fan : fan + 1, 0:share] = (own & 255).astype(F32)
    rows[fan : fan + 1, 128 : 128 + share] = (own >> 8).astype(F32)
    rows[fan + 1 : fan + 2, 0:share] = count_ref[...].astype(F32)
    rows[fan + 2 : fan + 4, 0:pairs] = (pairs_ref[...] & 255).astype(F32)
    rows[fan + 2 : fan + 4, 128 : 128 + pairs] = (pairs_ref[...] >> 8).astype(F32)
    out_ref[0:width, :] = ws_ref[...]
    out_ref[width : 2 * width, :] = wn_ref[...]
    out_ref[2 * width :, :] = rows[...].astype(BF)


def pack(self_two, neigh_two, count_two, pairs, ws, wn, features_t, across):
    width, wide = ws.shape
    return pl.pallas_call(
        functools.partial(pack_kernel, across),
        out_shape=[
            jax.ShapeDtypeStruct((2 * width + 32, wide), BF),
            jax.ShapeDtypeStruct(features_t.shape, BF),
        ],
        scratch_shapes=[pltpu.VMEM((32, wide), F32)],
        compiler_params=pltpu.CompilerParams(vmem_limit_bytes=16 * 2**20),
        name="pack",
    )(self_two, neigh_two, count_two, pairs, ws, wn, features_t)


def count_blocks(keys_ref, lows_ref, base, out_ref, marks):
    chunks, _, chunk = out_ref.shape
    spans = chunks * chunk // 256
    across = chunk // 256

    def stretch(row, rows):
        small = jnp.broadcast_to(row, (16, 256)).astype(BF)
        return jnp.concatenate([small] * (rows // 16), axis=0)

    def block(pair, _):
        one = jnp.ones((256, 256), BF)
        zero = jnp.zeros((256, 256), BF)
        place = pl.multiple_of(pair * 32, 32)
        rights = []
        for at in (pair * 2, pair * 2 + 1):
            low = stretch(lows_ref[pl.ds(base + at, 1), :], 256)
            rights.append(jnp.where(low == marks[...], one, zero))
        for first in range(0, spans, 16):
            size = min(16, spans - first)
            parts = []
            for side in range(2):
                row = keys_ref[pl.ds(base + pair * 2 + side, 1), :]
                key = stretch(row - float(first * 16), size * 16)
                left = jnp.where(
                    key == marks[0 : size * 16, :], one[: size * 16], zero[: size * 16]
                )
                parts.append(dot(left, rights[side], NT))
            for inner in range(size):
                span = first + inner
                lane = (span % across) * 256
                rows = [part[inner * 16 : (inner + 1) * 16] for part in parts]
                out_ref[span // across, pl.ds(place, 32), lane : lane + 256] = jnp.concatenate(
                    rows, axis=0
                ).astype(out_ref.dtype)
        return 0

    lax.fori_loop(0, 8, block, 0, unroll=4)


def all_marks():
    return lax.broadcasted_iota(jnp.int32, (256, 256), 0).astype(F32).astype(BF)


def count_one_kernel(ids_ref, live_ref, out_ref, marks, keys, lows):
    fan = ids_ref.shape[0]

    @pl.when(pl.program_id(0) == 0)
    def _():
        marks[...] = all_marks()
        slots = lax.broadcasted_iota(jnp.int32, (fan, 128), 0)
        high = []
        low = []
        for node in range(16):
            ids = ids_ref[:, node * 128 : (node + 1) * 128]
            live = slots < live_ref[:, node * 128 : (node + 1) * 128]
            high.append(((ids >> 8) * 16 + node).astype(F32))
            low.append(jnp.where(live, ids & 255, -1).astype(F32))
        keys[...] = jnp.concatenate(high, axis=0).T
        lows[...] = jnp.concatenate(low, axis=0).T

    count_blocks(keys, lows, pl.program_id(0) * 16, out_ref, marks)


def count_one_matrix(ids, live, total, chunk):
    fan, nodes = ids.shape
    return pl.pallas_call(
        count_one_kernel,
        grid=(nodes // 256,),
        out_shape=jax.ShapeDtypeStruct((total // chunk, nodes, chunk), F8),
        in_specs=[
            pl.BlockSpec((fan, nodes), lambda at: (0, 0)),
            pl.BlockSpec((1, nodes), lambda at: (0, 0)),
        ],
        out_specs=pl.BlockSpec((total // chunk, 256, chunk), lambda at: (0, at, 0)),
        scratch_shapes=[
            pltpu.VMEM((256, 256), BF),
            pltpu.VMEM((128, 256), F32),
            pltpu.VMEM((128, 256), F32),
        ],
        compiler_params=pltpu.CompilerParams(vmem_limit_bytes=VMEM_LIMIT),
        cost_estimate=pl.CostEstimate(
            flops=2 * nodes * total * 256, bytes_accessed=nodes * total, transcendentals=0
        ),
        name="count_one",
    )(ids, live)


def count_two_kernel(keys_ref, lows_ref, out_ref, marks):
    @pl.when(pl.program_id(0) == 0)
    def _():
        marks[...] = all_marks()

    count_blocks(keys_ref, lows_ref, 0, out_ref, marks)


def count_two_matrix(keys, lows, total):
    nodes = keys.shape[0] * 16
    return pl.pallas_call(
        count_two_kernel,
        grid=(nodes // 256,),
        out_shape=jax.ShapeDtypeStruct((1, nodes, total), BF),
        in_specs=[
            pl.BlockSpec((16, 256), lambda at: (at, 0)),
            pl.BlockSpec((16, 256), lambda at: (at, 0)),
        ],
        out_specs=pl.BlockSpec((1, 256, total), lambda at: (0, at, 0)),
        scratch_shapes=[pltpu.VMEM((256, 256), BF)],
        compiler_params=pltpu.CompilerParams(vmem_limit_bytes=VMEM_LIMIT),
        cost_estimate=pl.CostEstimate(
            flops=2 * nodes * total * 256, bytes_accessed=2 * nodes * total, transcendentals=0
        ),
        name="count_two",
    )(keys, lows)


def hop_kernel(
    steps, self_ref, counts_ref, front_ref, out_ref, table, total, own, up, down, live
):
    owners, width, cap = front_ref.shape
    blocks, _, block = out_ref.shape
    step = pl.program_id(0)
    per = owners // steps
    half = steps // 2
    across = blocks * block // 128

    @pl.when(step == 0)
    def _():
        most = jnp.abs(front_ref[0])
        for owner in range(1, owners):
            most = jnp.maximum(most, jnp.abs(front_ref[owner]))
        most = jnp.max(most.astype(F32), axis=1, keepdims=True)
        power = jnp.ones_like(most)
        back = jnp.ones_like(most)
        for exponent in (32, 32, 16, 16, 8, 4, 2, 1):
            fits = most * power * 2.0**exponent <= 224.0
            power = jnp.where(fits, power * 2.0**exponent, power)
            back = jnp.where(fits, back * 2.0**-exponent, back)
        up[...] = jnp.broadcast_to(power, up.shape)
        down[...] = jnp.broadcast_to(back, down.shape)
        total[...] = jnp.zeros_like(total)
        live[...] = jnp.zeros_like(live)

    def product():
        front = jnp.concatenate([front_ref[step * per + at] for at in range(per)], axis=1)
        front = front.astype(F32) * up[:, 0:1]
        high = front.astype(F8)
        low = ((front - high.astype(F32)) * 16.0).astype(F8)
        ones = jnp.ones((32, front.shape[1]), F8)
        part = dot(jnp.concatenate([high, low, ones], axis=0), counts_ref[0], NT)
        total[...] += part[:width] + part[width : 2 * width] * (1.0 / 16.0)
        live[...] += part[2 * width : 2 * width + 8]

    @pl.when(step < half)
    def _():
        for at in range(owners // half):
            owner = step * (owners // half) + at
            place = pl.multiple_of(owner * cap, cap)
            table[pl.ds(place, cap), 0:width] = front_ref[owner].astype(F32).T
        product()

    @pl.when(step >= half)
    def _():
        for at in range(blocks // half):
            dest = (step - half) * (blocks // half) + at
            for row in range(block):
                place = at * block + row
                node = row % across * 128 + dest * (block // across) + row // across
                own[place : place + 1, :] = table[pl.ds(self_ref[node], 1), :]
            rows = own[at * block : (at + 1) * block, 0:width]
            out_ref[dest, 0:width, :] = rows.T.astype(BF)
        product()

    @pl.when(step == steps - 1)
    def _():
        back = down[:, 0:1]
        inv = 1.0 / live[0:1, :]
        for dest in range(blocks):
            mean = total[:, dest * block : (dest + 1) * block] * back
            mean = mean * inv[:, dest * block : (dest + 1) * block]
            out_ref[dest, width : 2 * width, :] = mean.astype(BF)


def hop(frontier, counts, self_ids, blocks):
    owners, width, cap = frontier.shape
    chunks, nodes, chunk = counts.shape
    block = nodes // blocks
    return pl.pallas_call(
        functools.partial(hop_kernel, chunks),
        grid=(chunks,),
        out_shape=jax.ShapeDtypeStruct((blocks, 2 * width, block), BF),
        in_specs=[
            pl.BlockSpec(memory_space=pltpu.SMEM),
            pl.BlockSpec((1, nodes, chunk), lambda at: (at, 0, 0)),
            pl.BlockSpec((owners, width, cap), lambda at: (0, 0, 0)),
        ],
        out_specs=pl.BlockSpec((blocks, 2 * width, block), lambda at: (0, 0, 0)),
        scratch_shapes=[
            pltpu.VMEM((owners * cap, 128), F32),
            pltpu.VMEM((width, nodes), F32),
            pltpu.VMEM((nodes * 2 // chunks, 128), F32),
            pltpu.VMEM((width, 128), F32),
            pltpu.VMEM((width, 128), F32),
            pltpu.VMEM((8, nodes), F32),
        ],
        compiler_params=pltpu.CompilerParams(vmem_limit_bytes=VMEM_LIMIT),
        cost_estimate=pl.CostEstimate(
            flops=2 * nodes * chunks * chunk * 128,
            bytes_accessed=nodes * chunks * chunk,
            transcendentals=0,
        ),
        name="first_hop",
    )(self_ids, counts, frontier)


def first_kernel(side, me_ref, mine_ref, *refs):
    early_refs, (out_ref, fields_ref) = refs[:side], refs[side:]
    _, depth, block = mine_ref.shape
    row, column = me_ref[0], me_ref[1]
    weights = []
    mine = []
    for far in range(side):
        for near in range(side):
            owner = lax.rem(row + side - far, side) * side + lax.rem(column + side - near, side)
            weights.append(early_refs[far][near, 0:depth, :])
            mine.append(mine_ref[owner])
            fields_ref[owner] = early_refs[far][near, depth:, :].astype(F32)
    pre = dot(jnp.concatenate(weights, axis=0), jnp.concatenate(mine, axis=0), TN)
    hidden = jnp.maximum(pre, 0.0).astype(BF)
    for at in range(out_ref.shape[0]):
        out_ref[at] = hidden


def first(mine, early, me):
    feats, depth, block = mine.shape
    side, rows, wide = early[0].shape
    vm = pl.BlockSpec(memory_space=pltpu.VMEM)
    return pl.pallas_call(
        functools.partial(first_kernel, side),
        out_shape=[
            jax.ShapeDtypeStruct((feats, wide, block), BF),
            jax.ShapeDtypeStruct((feats, rows - depth, wide), F32),
        ],
        in_specs=[pl.BlockSpec(memory_space=pltpu.SMEM)] + [vm] * (1 + side),
        out_specs=[vm, vm],
        compiler_params=pltpu.CompilerParams(vmem_limit_bytes=VMEM_LIMIT),
        name="first_layer",
    )(me, mine, *early)


def mark_rows(ids_ref, out_ref, marks):
    total, count = out_ref.shape
    one = jnp.ones((256, count), BF); zero = jnp.zeros((256, count), BF)
    for first in range(0, total, 256):
        row = jnp.broadcast_to(ids_ref[...] - float(first), (16, count)).astype(BF)
        row = jnp.concatenate([row] * 16, axis=0)
        out_ref[first:first + 256, :] = jnp.where(row == marks, one, zero)

def second_kernel(scale, negative_total, hidden_ref, rows_ref, self_ref, ends_ref, inv_ref, ws_ref, wn_ref, neigh_hbm,
                  out_ref, neigh, own, ends, hidden_t, sem):
    copy = pltpu.make_async_copy(neigh_hbm, neigh, sem)
    copy.start()
    blocks, width, block = hidden_ref.shape
    for at in range(blocks):
        hidden_t[:, at * block:(at + 1) * block] = hidden_ref[at]
    targets = own.shape[1]
    marks = lax.broadcasted_iota(jnp.int32, (256, targets), 0).astype(F32).astype(BF)
    mark_rows(self_ref, own, marks)
    mark_rows(ends_ref, ends, marks)
    inv = inv_ref[...]
    hidden = hidden_t[...]
    hs = dot(hidden, own[...], NN).astype(BF)
    copy.wait()
    hn = (dot(hidden, neigh[...], NT) * inv).astype(BF)
    embed = (dot(ws_ref[...], hs, TN) + dot(wn_ref[...], hn, TN)).astype(BF)
    rows = dot(embed, ends[...], NN).astype(BF)
    count = rows.shape[1] // 3
    source, dest, negative = rows[:, :count], rows[:, count:2 * count], rows[:, 2 * count:]
    pos = jnp.sum(source.astype(F32) * dest.astype(F32), axis=0, keepdims=True) * scale
    neg = dot(source, negative, TN) * scale
    small = jnp.exp(-jnp.abs(neg))
    neg_sig = jnp.where(neg >= 0, 1.0, small) / (1.0 + small)
    neg_loss = jnp.maximum(neg, 0.0) + jnp.log1p(small)
    small = jnp.exp(-jnp.abs(pos))
    pos_grad = -(jnp.where(pos >= 0, small, 1.0) / (1.0 + small))
    pos_loss = jnp.maximum(-pos, 0.0) + jnp.log1p(small)
    loss = jnp.sum(neg_loss, axis=0, keepdims=True) * (1.0 / negative_total) + pos_loss
    loss = jnp.sum(loss, axis=1, keepdims=True)
    neg_grad = (neg_sig * (1.0 / negative_total)).astype(BF)
    source_grad = (pos_grad * dest.astype(F32) + dot(negative, neg_grad, NT)) * scale
    dest_grad = pos_grad * source.astype(F32) * scale
    negative_grad = dot(source, neg_grad, NN) * scale
    grads = jnp.concatenate([source_grad.astype(BF), dest_grad.astype(BF), negative_grad.astype(BF)], axis=1)
    eg = dot(grads, ends[...], NT).astype(BF)
    groups = out_ref.shape[0]
    many = 2 * ws_ref.shape[0] // groups
    sums = jnp.concatenate([dot(hs, eg, NT), dot(hn, eg, NT)], axis=0).astype(BF)
    for group in range(groups):
        out_ref[group, 0:many, :] = sums[group * many : (group + 1) * many]
    self_back = dot(ws_ref[...], eg, NN).astype(BF)
    neigh_back = (dot(wn_ref[...], eg, NN) * inv).astype(BF)
    hidden_grad = dot(self_back, own[...], NT) + dot(neigh_back, neigh[...], NN)
    pre = jnp.where(hidden > 0, hidden_grad, 0.0).astype(BF)
    rows_one = jnp.concatenate([rows_ref[at] for at in range(blocks)], axis=1)
    part = dot(rows_one, pre, NT)
    few = part.shape[0] // groups
    high = loss.astype(BF).astype(F32)
    mid = (loss - high).astype(BF).astype(F32)
    low = loss - high - mid
    lanes = lax.broadcasted_iota(jnp.int32, (8 - few, part.shape[1]), 1)
    tail = jnp.where(lanes == 0, high, jnp.where(lanes == 1, mid, low))
    for group in range(groups):
        rows = jnp.concatenate([part[group * few : (group + 1) * few], tail], axis=0)
        out_ref[group, many : many + 8, :] = rows.astype(BF)


def second(
    hidden, rows_one, pick_neigh, self_two, ends, inv, ws, wn, scale, negative_total, groups
):
    blocks, width, block = hidden.shape
    nodes = blocks * block
    targets = self_two.shape[1]
    many = ends.shape[1]
    vm = pl.BlockSpec(memory_space=pltpu.VMEM)
    return pl.pallas_call(functools.partial(second_kernel, scale, negative_total),
        out_shape=jax.ShapeDtypeStruct((groups, 2 * width // groups + 8, width), BF),
        in_specs=[vm] * 7 + [pl.BlockSpec(memory_space=pl.ANY)],
        out_specs=vm,
        scratch_shapes=[pltpu.VMEM((targets, nodes), BF), pltpu.VMEM((nodes, targets), BF), pltpu.VMEM((targets, many), BF), pltpu.VMEM((width, nodes), BF), pltpu.SemaphoreType.DMA],
        compiler_params=pltpu.CompilerParams(vmem_limit_bytes=VMEM_LIMIT),
        name="second_layer")(hidden, rows_one, self_two, ends, inv, ws, wn, pick_neigh)

def local(
    features,
    frontier_ids,
    self_one_ids,
    neigh_one_ids,
    count_one,
    self_two_ids,
    neigh_two_ids,
    count_two,
    pos_pairs,
    neg_ids,
    first_self,
    first_neigh,
    second_self,
    second_neigh,
):
    graphs = lax.axis_size("graph")
    feats = lax.axis_size("feat")
    hidden_width = second_self.shape[0]
    scale = 1.0 / math.sqrt(hidden_width)
    negative_total = neg_ids.shape[1]
    nodes = self_one_ids.shape[1]
    fan = neigh_one_ids.shape[1]
    width = features.shape[1]
    cap = frontier_ids.shape[2]
    front = graphs * cap
    share = self_two_ids.shape[1]
    pair_share = pos_pairs.shape[2]

    asked = swap(frontier_ids[0], "graph")

    early, features_t = pack(
        self_two_ids,
        neigh_two_ids[0],
        count_two,
        pos_pairs[0],
        first_self,
        first_neigh,
        features.T,
        nodes // 128,
    )
    side = math.isqrt(feats)
    me = lax.axis_index("feat")
    me = jnp.stack([me // side, me % side]).astype(jnp.int32)
    along = [
        [(at, at // side * side + (at + far) % side) for at in range(feats)]
        for far in range(1, side)
    ]
    across = [
        [(at, (at + far * side) % feats) for at in range(feats)] for far in range(1, side)
    ]
    asked, early = lax.optimization_barrier((asked, early))
    early = jnp.stack([early] + [lax.ppermute(early, "feat", pairs) for pairs in along])
    served = serve(features_t, asked.reshape(-1), graphs, cap)
    one_ids, served, early = lax.optimization_barrier((neigh_one_ids[0], served, early))
    early = [early] + [lax.ppermute(early, "feat", pairs) for pairs in across]
    one_counts = count_one_matrix(one_ids, count_one, front, 2 * cap)
    frontier = swap(served, "graph")
    frontier, early = lax.optimization_barrier((frontier, early))
    rows_one = hop(frontier, one_counts, self_one_ids[0], feats)
    hidden, sent = first(swap(rows_one, "feat"), early, me)
    hidden = swap(hidden, "feat")

    def blocks(value):
        value = value.reshape(feats, fan, share // 16, 16).transpose(0, 2, 1, 3)
        return value.reshape(-1, fan * 16)

    node = (lax.broadcasted_iota(jnp.int32, (feats, fan, share), 2) % 16).astype(F32)
    keys = blocks(sent[:, :fan, 128 : 128 + share] * 16.0 + node)
    pick_neigh = count_two_matrix(keys, blocks(sent[:, :fan, :share]), nodes)[0]
    self_two = sent[:, fan, :share] + sent[:, fan, 128 : 128 + share] * 256.0
    self_two = self_two.reshape(1, -1)
    inv_two = 1.0 / sent[:, fan + 1, :share].reshape(1, -1)
    pairs = sent[:, fan + 2 : fan + 4]
    pairs = pairs[:, :, :pair_share] + pairs[:, :, 128 : 128 + pair_share] * 256.0
    pairs = pairs.transpose(1, 0, 2)
    pair_total = feats * pair_share
    ends = jnp.concatenate([pairs.reshape(1, -1), neg_ids.astype(F32)], axis=1)
    parts = second(
        hidden,
        rows_one,
        pick_neigh,
        self_two,
        ends,
        inv_two,
        second_self,
        second_neigh,
        scale,
        negative_total,
        graphs,
    )

    sums = jnp.sum(swap(parts, "graph").astype(F32), axis=0)
    loss = jnp.sum(sums[-1, 0:3])
    whole = gather_all(sums.astype(BF), "graph").astype(F32)
    second_rows = 2 * hidden_width // graphs
    first_rows = 2 * width // graphs
    second_sums = whole[:, :second_rows].reshape(2 * hidden_width, hidden_width)
    first_sums = whole[:, second_rows : second_rows + first_rows].reshape(-1, hidden_width)
    return (
        first_sums[:width],
        first_sums[width:],
        second_sums[:hidden_width],
        second_sums[hidden_width:],
        loss / (pair_total * graphs),
    )


def solution(mesh):
    placed = (
        P("graph", "feat"),
        P("graph", None, None),
        P("graph", None),
        P("graph", None, None),
        P("graph", None),
        P("graph", "feat"),
        P("graph", None, "feat"),
        P("graph", "feat"),
        P("graph", None, "feat"),
        P("graph", None),
        P("feat", None),
        P("feat", None),
        P(),
        P(),
    )
    return jax.shard_map(
        local,
        mesh=mesh,
        in_specs=placed,
        out_specs=(P("feat", None), P("feat", None), P(), P(), P()),
        check_vma=False,
    )
```

```python
import functools
import math

import jax
import jax.numpy as jnp
from jax import lax
from jax.experimental import pallas as pl
from jax.experimental.pallas import tpu as pltpu
from jax.sharding import PartitionSpec as P

BF = jnp.bfloat16
F32 = jnp.float32
F8 = jnp.float8_e4m3fn
VMEM_LIMIT = 50 * 2**20
NN = ((1,), (0,))
NT = ((1,), (1,))
TN = ((0,), (0,))


def swap(value, axis):
    return lax.all_to_all(value, axis, split_axis=0, concat_axis=0, tiled=True)


def gather_all(value, axis):
    size = lax.axis_size(axis)
    return swap(jnp.broadcast_to(value[None], (size,) + value.shape), axis)


def in_hbm(value):
    return pltpu.with_memory_space_constraint(value, pltpu.HBM)


def dot(former, latter, dims):
    return lax.dot_general(former, latter, (dims, ((), ())), preferred_element_type=F32)


def serve_kernel(ids_ref, feat_ref, out_ref, table, picked):
    width, rows = feat_ref.shape
    groups, _, cap = out_ref.shape
    step = 512

    def fill(at, _):
        at = pl.multiple_of(at * step, step)
        table[pl.ds(at, step), 0:width] = feat_ref[:, pl.ds(at, step)].astype(F32).T
        return 0

    lax.fori_loop(0, rows // step, fill, 0)

    def take(group, side):
        for row in range(0, cap, 8):
            rows = [
                table[pl.ds(ids_ref[group * cap + row + at], 1), :] for at in range(8)
            ]
            picked[side, row : row + 8, :] = jnp.concatenate(rows, axis=0)

    def put(group, side):
        out_ref[group] = picked[side, :, 0:width].T.astype(out_ref.dtype)

    def two(at, _):
        group = at * 2 + 1
        take(group, 1)
        put(group - 1, 0)
        take(group + 1, 0)
        put(group, 1)
        return 0

    take(0, 0)
    lax.fori_loop(0, groups // 2 - 1, two, 0)
    take(groups - 1, 1)
    put(groups - 2, 0)
    put(groups - 1, 1)


def serve(features_t, ids, groups, cap):
    width, rows = features_t.shape
    return pl.pallas_call(
        serve_kernel,
        out_shape=jax.ShapeDtypeStruct((groups, width, cap), features_t.dtype),
        in_specs=[
            pl.BlockSpec(memory_space=pltpu.SMEM),
            pl.BlockSpec(memory_space=pltpu.VMEM),
        ],
        out_specs=pl.BlockSpec(memory_space=pltpu.VMEM),
        scratch_shapes=[pltpu.VMEM((rows, 128), F32), pltpu.VMEM((2, cap, 128), F32)],
        compiler_params=pltpu.CompilerParams(vmem_limit_bytes=VMEM_LIMIT),
        name="serve",
    )(ids, features_t)


def pack_kernel(across, *refs):
    sources, (out_ref, copy_ref), held, rows, sems = refs[:7], refs[7:9], refs[9:15], refs[15], refs[16]
    copies = [
        pltpu.make_async_copy(source, place, sems.at[at])
        for at, (source, place) in enumerate(zip(sources, [*held, copy_ref]))
    ]
    for copy in copies:
        copy.start()
    for copy in copies:
        copy.wait()
    self_ref, neigh_ref, count_ref, pairs_ref, ws_ref, wn_ref = held
    width = ws_ref.shape[0]
    fan, share = neigh_ref.shape
    pairs = pairs_ref.shape[1]

    def place(ids):
        return (ids & 127) * across + (ids >> 7)

    rows[...] = jnp.zeros_like(rows)
    neigh = place(neigh_ref[...])
    live = lax.broadcasted_iota(jnp.int32, (fan, share), 0) < count_ref[...]
    rows[0:fan, 0:share] = jnp.where(live, neigh & 255, -1).astype(F32)
    rows[0:fan, 128 : 128 + share] = (neigh >> 8).astype(F32)
    own = place(self_ref[...])
    rows[fan : fan + 1, 0:share] = (own & 255).astype(F32)
    rows[fan : fan + 1, 128 : 128 + share] = (own >> 8).astype(F32)
    rows[fan + 1 : fan + 2, 0:share] = count_ref[...].astype(F32)
    rows[fan + 2 : fan + 4, 0:pairs] = (pairs_ref[...] & 255).astype(F32)
    rows[fan + 2 : fan + 4, 128 : 128 + pairs] = (pairs_ref[...] >> 8).astype(F32)
    out_ref[0:width, :] = ws_ref[...]
    out_ref[width : 2 * width, :] = wn_ref[...]
    out_ref[2 * width :, :] = rows[...].astype(BF)


def pack(self_two, neigh_two, count_two, pairs, ws, wn, features_t, across):
    width, wide = ws.shape
    operands = (self_two, neigh_two, count_two, pairs, ws, wn, features_t)
    held = [pltpu.VMEM(value.shape, value.dtype) for value in operands[:6]]
    return pl.pallas_call(
        functools.partial(pack_kernel, across),
        out_shape=[
            jax.ShapeDtypeStruct((2 * width + 32, wide), BF),
            jax.ShapeDtypeStruct(features_t.shape, BF),
        ],
        in_specs=[pl.BlockSpec(memory_space=pl.ANY)] * len(operands),
        out_specs=[pl.BlockSpec(memory_space=pltpu.VMEM)] * 2,
        scratch_shapes=[
            *held,
            pltpu.VMEM((32, wide), F32),
            pltpu.SemaphoreType.DMA((len(operands),)),
        ],
        compiler_params=pltpu.CompilerParams(vmem_limit_bytes=16 * 2**20),
        name="pack",
    )(*(in_hbm(value) for value in operands))


def count_blocks(keys_ref, lows_ref, base, out_ref, marks):
    chunks, _, chunk = out_ref.shape
    spans = chunks * chunk // 256
    across = chunk // 256

    def stretch(row, rows):
        small = jnp.broadcast_to(row, (16, 256)).astype(BF)
        return jnp.concatenate([small] * (rows // 16), axis=0)

    def block(pair, _):
        one = jnp.ones((256, 256), BF)
        zero = jnp.zeros((256, 256), BF)
        place = pl.multiple_of(pair * 32, 32)
        rights = []
        for at in (pair * 2, pair * 2 + 1):
            low = stretch(lows_ref[pl.ds(base + at, 1), :], 256)
            rights.append(jnp.where(low == marks[...], one, zero))
        for first in range(0, spans, 16):
            size = min(16, spans - first)
            parts = []
            for side in range(2):
                row = keys_ref[pl.ds(base + pair * 2 + side, 1), :]
                key = stretch(row - float(first * 16), size * 16)
                left = jnp.where(
                    key == marks[0 : size * 16, :], one[: size * 16], zero[: size * 16]
                )
                parts.append(dot(left, rights[side], NT))
            for inner in range(size):
                span = first + inner
                lane = (span % across) * 256
                rows = [part[inner * 16 : (inner + 1) * 16] for part in parts]
                out_ref[span // across, pl.ds(place, 32), lane : lane + 256] = jnp.concatenate(
                    rows, axis=0
                ).astype(out_ref.dtype)
        return 0

    lax.fori_loop(0, 8, block, 0, unroll=4)


def all_marks():
    return lax.broadcasted_iota(jnp.int32, (256, 256), 0).astype(F32).astype(BF)


def count_one_kernel(ids_from, live_from, out_ref, marks, keys, lows, ids_ref, live_ref, sems):
    fan = ids_ref.shape[0]

    @pl.when(pl.program_id(0) == 0)
    def _():
        first = pltpu.make_async_copy(ids_from, ids_ref, sems.at[0])
        other = pltpu.make_async_copy(live_from, live_ref, sems.at[1])
        first.start()
        other.start()
        marks[...] = all_marks()
        first.wait()
        other.wait()
        slots = lax.broadcasted_iota(jnp.int32, (fan, 128), 0)
        high = []
        low = []
        for node in range(16):
            ids = ids_ref[:, node * 128 : (node + 1) * 128]
            live = slots < live_ref[:, node * 128 : (node + 1) * 128]
            high.append(((ids >> 8) * 16 + node).astype(F32))
            low.append(jnp.where(live, ids & 255, -1).astype(F32))
        keys[...] = jnp.concatenate(high, axis=0).T
        lows[...] = jnp.concatenate(low, axis=0).T

    count_blocks(keys, lows, pl.program_id(0) * 16, out_ref, marks)


def count_one_matrix(ids, live, total, chunk):
    fan, nodes = ids.shape
    return pl.pallas_call(
        count_one_kernel,
        grid=(nodes // 256,),
        out_shape=jax.ShapeDtypeStruct((total // chunk, nodes, chunk), F8),
        in_specs=[pl.BlockSpec(memory_space=pl.ANY)] * 2,
        out_specs=pl.BlockSpec((total // chunk, 256, chunk), lambda at: (0, at, 0)),
        scratch_shapes=[
            pltpu.VMEM((256, 256), BF),
            pltpu.VMEM((128, 256), F32),
            pltpu.VMEM((128, 256), F32),
            pltpu.VMEM((fan, nodes), jnp.int32),
            pltpu.VMEM((1, nodes), jnp.int32),
            pltpu.SemaphoreType.DMA((2,)),
        ],
        compiler_params=pltpu.CompilerParams(vmem_limit_bytes=VMEM_LIMIT),
        cost_estimate=pl.CostEstimate(
            flops=2 * nodes * total * 256, bytes_accessed=nodes * total, transcendentals=0
        ),
        name="count_one",
    )(in_hbm(ids), in_hbm(live))


def count_two_kernel(fan, sent_ref, out_ref, marks, keys, lows):
    @pl.when(pl.program_id(0) == 0)
    def _():
        marks[...] = all_marks()
        high = []
        low = []
        for device in range(sent_ref.shape[0]):
            low.append(sent_ref[device, 0:fan, 0:128])
            high.append(sent_ref[device, 0:fan, 128:256] * 16.0 + float(device))
        keys[...] = jnp.concatenate(high, axis=0).T
        lows[...] = jnp.concatenate(low, axis=0).T

    count_blocks(keys, lows, pl.program_id(0) * 16, out_ref, marks)


def count_two_matrix(sent, fan, share, total):
    nodes = sent.shape[0] * share
    return pl.pallas_call(
        functools.partial(count_two_kernel, fan),
        grid=(nodes // 256,),
        out_shape=jax.ShapeDtypeStruct((1, nodes, total), BF),
        in_specs=[pl.BlockSpec(sent.shape, lambda at: (0, 0, 0))],
        out_specs=pl.BlockSpec((1, 256, total), lambda at: (0, at, 0)),
        scratch_shapes=[
            pltpu.VMEM((256, 256), BF),
            pltpu.VMEM((128, 256), F32),
            pltpu.VMEM((128, 256), F32),
        ],
        compiler_params=pltpu.CompilerParams(vmem_limit_bytes=VMEM_LIMIT),
        cost_estimate=pl.CostEstimate(
            flops=2 * nodes * total * 256, bytes_accessed=2 * nodes * total, transcendentals=0
        ),
        name="count_two",
    )(sent)


def hop_kernel(
    steps, self_ref, counts_ref, front_ref, out_ref, table, total, own, up, down, live
):
    owners, width, cap = front_ref.shape
    blocks, _, block = out_ref.shape
    step = pl.program_id(0)
    per = owners // steps
    half = steps // 2
    across = blocks * block // 128

    @pl.when(step == 0)
    def _():
        most = jnp.abs(front_ref[0])
        for owner in range(1, owners):
            most = jnp.maximum(most, jnp.abs(front_ref[owner]))
        most = jnp.max(most.astype(F32), axis=1, keepdims=True)
        power = jnp.ones_like(most)
        back = jnp.ones_like(most)
        for exponent in (32, 32, 16, 16, 8, 4, 2, 1):
            fits = most * power * 2.0**exponent <= 224.0
            power = jnp.where(fits, power * 2.0**exponent, power)
            back = jnp.where(fits, back * 2.0**-exponent, back)
        up[...] = jnp.broadcast_to(power, up.shape)
        down[...] = jnp.broadcast_to(back, down.shape)
        total[...] = jnp.zeros_like(total)
        live[...] = jnp.zeros_like(live)

    def product():
        front = jnp.concatenate([front_ref[step * per + at] for at in range(per)], axis=1)
        front = front.astype(F32) * up[:, 0:1]
        high = front.astype(F8)
        low = ((front - high.astype(F32)) * 16.0).astype(F8)
        ones = jnp.ones((32, front.shape[1]), F8)
        part = dot(jnp.concatenate([high, low, ones], axis=0), counts_ref[0], NT)
        total[...] += part[:width] + part[width : 2 * width] * (1.0 / 16.0)
        live[...] += part[2 * width : 2 * width + 8]

    @pl.when(step < half)
    def _():
        for at in range(owners // half):
            owner = step * (owners // half) + at
            place = pl.multiple_of(owner * cap, cap)
            table[pl.ds(place, cap), 0:width] = front_ref[owner].astype(F32).T
        product()

    @pl.when(step >= half)
    def _():
        for at in range(blocks // half):
            dest = (step - half) * (blocks // half) + at
            for row in range(block):
                place = at * block + row
                node = row % across * 128 + dest * (block // across) + row // across
                own[place : place + 1, :] = table[pl.ds(self_ref[node], 1), :]
            rows = own[at * block : (at + 1) * block, 0:width]
            out_ref[dest, 0:width, :] = rows.T.astype(BF)
        product()

    @pl.when(step == steps - 1)
    def _():
        back = down[:, 0:1]
        inv = 1.0 / live[0:1, :]
        for dest in range(blocks):
            mean = total[:, dest * block : (dest + 1) * block] * back
            mean = mean * inv[:, dest * block : (dest + 1) * block]
            out_ref[dest, width : 2 * width, :] = mean.astype(BF)


def hop(frontier, counts, self_ids, blocks):
    owners, width, cap = frontier.shape
    chunks, nodes, chunk = counts.shape
    block = nodes // blocks
    return pl.pallas_call(
        functools.partial(hop_kernel, chunks),
        grid=(chunks,),
        out_shape=jax.ShapeDtypeStruct((blocks, 2 * width, block), BF),
        in_specs=[
            pl.BlockSpec(memory_space=pltpu.SMEM),
            pl.BlockSpec((1, nodes, chunk), lambda at: (at, 0, 0)),
            pl.BlockSpec((owners, width, cap), lambda at: (0, 0, 0)),
        ],
        out_specs=pl.BlockSpec((blocks, 2 * width, block), lambda at: (0, 0, 0)),
        scratch_shapes=[
            pltpu.VMEM((owners * cap, 128), F32),
            pltpu.VMEM((width, nodes), F32),
            pltpu.VMEM((nodes * 2 // chunks, 128), F32),
            pltpu.VMEM((width, 128), F32),
            pltpu.VMEM((width, 128), F32),
            pltpu.VMEM((8, nodes), F32),
        ],
        compiler_params=pltpu.CompilerParams(vmem_limit_bytes=VMEM_LIMIT),
        cost_estimate=pl.CostEstimate(
            flops=2 * nodes * chunks * chunk * 128,
            bytes_accessed=nodes * chunks * chunk,
            transcendentals=0,
        ),
        name="first_hop",
    )(self_ids, counts, frontier)


def first_kernel(side, me_ref, mine_ref, *refs):
    early_refs, (out_ref, fields_ref) = refs[:side], refs[side:]
    _, depth, block = mine_ref.shape
    row, column = me_ref[0], me_ref[1]
    weights = []
    mine = []
    for far in range(side):
        for near in range(side):
            owner = lax.rem(row + side - far, side) * side + lax.rem(column + side - near, side)
            weights.append(early_refs[far][near, 0:depth, :])
            mine.append(mine_ref[owner])
            fields_ref[owner] = early_refs[far][near, depth:, :].astype(F32)
    pre = dot(jnp.concatenate(weights, axis=0), jnp.concatenate(mine, axis=0), TN)
    hidden = jnp.maximum(pre, 0.0).astype(BF)
    for at in range(out_ref.shape[0]):
        out_ref[at] = hidden


def first(mine, early, me):
    feats, depth, block = mine.shape
    side, rows, wide = early[0].shape
    vm = pl.BlockSpec(memory_space=pltpu.VMEM)
    return pl.pallas_call(
        functools.partial(first_kernel, side),
        out_shape=[
            jax.ShapeDtypeStruct((feats, wide, block), BF),
            jax.ShapeDtypeStruct((feats, rows - depth, wide), F32),
        ],
        in_specs=[pl.BlockSpec(memory_space=pltpu.SMEM)] + [vm] * (1 + side),
        out_specs=[vm, vm],
        compiler_params=pltpu.CompilerParams(vmem_limit_bytes=VMEM_LIMIT),
        name="first_layer",
    )(me, mine, *early)


def mark_rows(ids_ref, out_ref, marks):
    total, count = out_ref.shape
    one = jnp.ones((256, count), BF); zero = jnp.zeros((256, count), BF)
    for first in range(0, total, 256):
        row = jnp.broadcast_to(ids_ref[...] - float(first), (16, count)).astype(BF)
        row = jnp.concatenate([row] * 16, axis=0)
        out_ref[first:first + 256, :] = jnp.where(row == marks, one, zero)

def second_kernel(scale, negative_total, hidden_ref, rows_ref, self_ref, ends_ref, inv_ref, ws_ref, wn_ref, neigh_hbm,
                  out_ref, neigh, own, ends, hidden_t, sem):
    copy = pltpu.make_async_copy(neigh_hbm, neigh, sem)
    copy.start()
    blocks, width, block = hidden_ref.shape
    for at in range(blocks):
        hidden_t[:, at * block:(at + 1) * block] = hidden_ref[at]
    targets = own.shape[1]
    marks = lax.broadcasted_iota(jnp.int32, (256, targets), 0).astype(F32).astype(BF)
    mark_rows(self_ref, own, marks)
    mark_rows(ends_ref, ends, marks)
    inv = inv_ref[...]
    hidden = hidden_t[...]
    hs = dot(hidden, own[...], NN).astype(BF)
    copy.wait()
    hn = (dot(hidden, neigh[...], NT) * inv).astype(BF)
    embed = (dot(ws_ref[...], hs, TN) + dot(wn_ref[...], hn, TN)).astype(BF)
    rows = dot(embed, ends[...], NN).astype(BF)
    count = rows.shape[1] // 3
    source, dest, negative = rows[:, :count], rows[:, count:2 * count], rows[:, 2 * count:]
    pos = jnp.sum(source.astype(F32) * dest.astype(F32), axis=0, keepdims=True) * scale
    neg = dot(source, negative, TN) * scale
    small = jnp.exp(-jnp.abs(neg))
    neg_sig = jnp.where(neg >= 0, 1.0, small) / (1.0 + small)
    neg_loss = jnp.maximum(neg, 0.0) + jnp.log1p(small)
    small = jnp.exp(-jnp.abs(pos))
    pos_grad = -(jnp.where(pos >= 0, small, 1.0) / (1.0 + small))
    pos_loss = jnp.maximum(-pos, 0.0) + jnp.log1p(small)
    loss = jnp.sum(neg_loss, axis=0, keepdims=True) * (1.0 / negative_total) + pos_loss
    loss = jnp.sum(loss, axis=1, keepdims=True)
    neg_grad = (neg_sig * (1.0 / negative_total)).astype(BF)
    source_grad = (pos_grad * dest.astype(F32) + dot(negative, neg_grad, NT)) * scale
    dest_grad = pos_grad * source.astype(F32) * scale
    negative_grad = dot(source, neg_grad, NN) * scale
    grads = jnp.concatenate([source_grad.astype(BF), dest_grad.astype(BF), negative_grad.astype(BF)], axis=1)
    eg = dot(grads, ends[...], NT).astype(BF)
    groups = out_ref.shape[0]
    many = 2 * ws_ref.shape[0] // groups
    sums = jnp.concatenate([dot(hs, eg, NT), dot(hn, eg, NT)], axis=0).astype(BF)
    for group in range(groups):
        out_ref[group, 0:many, :] = sums[group * many : (group + 1) * many]
    self_back = dot(ws_ref[...], eg, NN).astype(BF)
    neigh_back = (dot(wn_ref[...], eg, NN) * inv).astype(BF)
    hidden_grad = dot(self_back, own[...], NT) + dot(neigh_back, neigh[...], NN)
    pre = jnp.where(hidden > 0, hidden_grad, 0.0).astype(BF)
    rows_one = jnp.concatenate([rows_ref[at] for at in range(blocks)], axis=1)
    part = dot(rows_one, pre, NT)
    few = part.shape[0] // groups
    high = loss.astype(BF).astype(F32)
    mid = (loss - high).astype(BF).astype(F32)
    low = loss - high - mid
    lanes = lax.broadcasted_iota(jnp.int32, (8 - few, part.shape[1]), 1)
    tail = jnp.where(lanes == 0, high, jnp.where(lanes == 1, mid, low))
    for group in range(groups):
        rows = jnp.concatenate([part[group * few : (group + 1) * few], tail], axis=0)
        out_ref[group, many : many + 8, :] = rows.astype(BF)


def second(
    hidden, rows_one, pick_neigh, self_two, ends, inv, ws, wn, scale, negative_total, groups
):
    blocks, width, block = hidden.shape
    nodes = blocks * block
    targets = self_two.shape[1]
    many = ends.shape[1]
    vm = pl.BlockSpec(memory_space=pltpu.VMEM)
    return pl.pallas_call(functools.partial(second_kernel, scale, negative_total),
        out_shape=jax.ShapeDtypeStruct((groups, 2 * width // groups + 8, width), BF),
        in_specs=[vm] * 7 + [pl.BlockSpec(memory_space=pl.ANY)],
        out_specs=vm,
        scratch_shapes=[pltpu.VMEM((targets, nodes), BF), pltpu.VMEM((nodes, targets), BF), pltpu.VMEM((targets, many), BF), pltpu.VMEM((width, nodes), BF), pltpu.SemaphoreType.DMA],
        compiler_params=pltpu.CompilerParams(vmem_limit_bytes=VMEM_LIMIT),
        name="second_layer")(hidden, rows_one, self_two, ends, inv, ws, wn, pick_neigh)

def local(
    features,
    frontier_ids,
    self_one_ids,
    neigh_one_ids,
    count_one,
    self_two_ids,
    neigh_two_ids,
    count_two,
    pos_pairs,
    neg_ids,
    first_self,
    first_neigh,
    second_self,
    second_neigh,
):
    graphs = lax.axis_size("graph")
    feats = lax.axis_size("feat")
    hidden_width = second_self.shape[0]
    scale = 1.0 / math.sqrt(hidden_width)
    negative_total = neg_ids.shape[1]
    nodes = self_one_ids.shape[1]
    fan = neigh_one_ids.shape[1]
    width = features.shape[1]
    cap = frontier_ids.shape[2]
    front = graphs * cap
    share = self_two_ids.shape[1]
    pair_share = pos_pairs.shape[2]

    asked = swap(frontier_ids[0], "graph")

    early, features_t = pack(
        self_two_ids,
        neigh_two_ids[0],
        count_two,
        pos_pairs[0],
        first_self,
        first_neigh,
        features.T,
        nodes // 128,
    )
    side = math.isqrt(feats)
    me = lax.axis_index("feat")
    me = jnp.stack([me // side, me % side]).astype(jnp.int32)
    along = [
        [(at, at // side * side + (at + far) % side) for at in range(feats)]
        for far in range(1, side)
    ]
    across = [
        [(at, (at + far * side) % feats) for at in range(feats)] for far in range(1, side)
    ]
    asked, early = lax.optimization_barrier((asked, early))
    early = jnp.stack([early] + [lax.ppermute(early, "feat", pairs) for pairs in along])
    served = serve(features_t, asked.reshape(-1), graphs, cap)
    one_ids, served, early = lax.optimization_barrier((neigh_one_ids[0], served, early))
    early = [early] + [lax.ppermute(early, "feat", pairs) for pairs in across]
    one_counts = count_one_matrix(one_ids, count_one, front, 2 * cap)
    frontier = swap(served, "graph")
    frontier, early = lax.optimization_barrier((frontier, early))
    rows_one = hop(frontier, one_counts, self_one_ids[0], feats)
    hidden, sent = first(swap(rows_one, "feat"), early, me)
    hidden = swap(hidden, "feat")

    pick_neigh = count_two_matrix(sent, fan, share, nodes)[0]
    self_two = sent[:, fan, :share] + sent[:, fan, 128 : 128 + share] * 256.0
    self_two = self_two.T.reshape(1, -1)
    inv_two = 1.0 / sent[:, fan + 1, :share].T.reshape(1, -1)
    pairs = sent[:, fan + 2 : fan + 4]
    pairs = pairs[:, :, :pair_share] + pairs[:, :, 128 : 128 + pair_share] * 256.0
    pairs = pairs.transpose(1, 0, 2)
    pair_total = feats * pair_share
    ends = jnp.concatenate([pairs.reshape(1, -1).astype(jnp.int32), neg_ids], axis=1)
    ends = (ends % share * feats + ends // share).astype(F32)
    parts = second(
        hidden,
        rows_one,
        pick_neigh,
        self_two,
        ends,
        inv_two,
        second_self,
        second_neigh,
        scale,
        negative_total,
        graphs,
    )

    sums = jnp.sum(swap(parts, "graph").astype(F32), axis=0)
    loss = jnp.sum(sums[-1, 0:3])
    whole = gather_all(sums.astype(BF), "graph").astype(F32)
    second_rows = 2 * hidden_width // graphs
    first_rows = 2 * width // graphs
    second_sums = whole[:, :second_rows].reshape(2 * hidden_width, hidden_width)
    first_sums = whole[:, second_rows : second_rows + first_rows].reshape(-1, hidden_width)
    return (
        first_sums[:width],
        first_sums[width:],
        second_sums[:hidden_width],
        second_sums[hidden_width:],
        loss / (pair_total * graphs),
    )


def solution(mesh):
    placed = (
        P("graph", "feat"),
        P("graph", None, None),
        P("graph", None),
        P("graph", None, None),
        P("graph", None),
        P("graph", "feat"),
        P("graph", None, "feat"),
        P("graph", "feat"),
        P("graph", None, "feat"),
        P("graph", None),
        P("feat", None),
        P("feat", None),
        P(),
        P(),
    )
    return jax.shard_map(
        local,
        mesh=mesh,
        in_specs=placed,
        out_specs=(P("feat", None), P("feat", None), P(), P(), P()),
        check_vma=False,
    )
```

```python
import functools
import math

import jax
import jax.numpy as jnp
from jax import lax
from jax.experimental import pallas as pl
from jax.experimental.pallas import tpu as pltpu
from jax.sharding import PartitionSpec as P

BF = jnp.bfloat16
F32 = jnp.float32
F8 = jnp.float8_e4m3fn
VMEM_LIMIT = 50 * 2**20
NN = ((1,), (0,))
NT = ((1,), (1,))
TN = ((0,), (0,))


def swap(value, axis):
    return lax.all_to_all(value, axis, split_axis=0, concat_axis=0, tiled=True)


def gather_all(value, axis):
    size = lax.axis_size(axis)
    return swap(jnp.broadcast_to(value[None], (size,) + value.shape), axis)


def in_hbm(value):
    return pltpu.with_memory_space_constraint(value, pltpu.HBM)


def dot(former, latter, dims):
    return lax.dot_general(former, latter, (dims, ((), ())), preferred_element_type=F32)


def serve_kernel(ids_ref, feat_ref, out_ref, table, picked):
    width, rows = feat_ref.shape
    groups, _, cap = out_ref.shape
    step = 512

    def fill(at, _):
        at = pl.multiple_of(at * step, step)
        table[pl.ds(at, step), 0:width] = feat_ref[:, pl.ds(at, step)].astype(F32).T
        return 0

    lax.fori_loop(0, rows // step, fill, 0)

    def take(group, side):
        for row in range(0, cap, 8):
            rows = [
                table[pl.ds(ids_ref[group * cap + row + at], 1), :] for at in range(8)
            ]
            picked[side, row : row + 8, :] = jnp.concatenate(rows, axis=0)

    def put(group, side):
        out_ref[group] = picked[side, :, 0:width].T.astype(out_ref.dtype)

    def two(at, _):
        group = at * 2 + 1
        take(group, 1)
        put(group - 1, 0)
        take(group + 1, 0)
        put(group, 1)
        return 0

    take(0, 0)
    lax.fori_loop(0, groups // 2 - 1, two, 0)
    take(groups - 1, 1)
    put(groups - 2, 0)
    put(groups - 1, 1)


def serve(features_t, ids, groups, cap):
    width, rows = features_t.shape
    return pl.pallas_call(
        serve_kernel,
        out_shape=jax.ShapeDtypeStruct((groups, width, cap), features_t.dtype),
        in_specs=[
            pl.BlockSpec(memory_space=pltpu.SMEM),
            pl.BlockSpec(memory_space=pltpu.VMEM),
        ],
        out_specs=pl.BlockSpec(memory_space=pltpu.VMEM),
        scratch_shapes=[pltpu.VMEM((rows, 128), F32), pltpu.VMEM((2, cap, 128), F32)],
        compiler_params=pltpu.CompilerParams(vmem_limit_bytes=VMEM_LIMIT),
        name="serve",
    )(ids, features_t)


def pack_kernel(across, *refs):
    sources, (out_ref, copy_ref), held, rows, sems = refs[:7], refs[7:9], refs[9:15], refs[15], refs[16]
    copies = [
        pltpu.make_async_copy(source, place, sems.at[at])
        for at, (source, place) in enumerate(zip(sources, [*held, copy_ref]))
    ]
    for copy in copies:
        copy.start()
    for copy in copies:
        copy.wait()
    self_ref, neigh_ref, count_ref, pairs_ref, ws_ref, wn_ref = held
    width = ws_ref.shape[0]
    fan, share = neigh_ref.shape
    pairs = pairs_ref.shape[1]

    def place(ids):
        return (ids & 127) * across + (ids >> 7)

    rows[...] = jnp.zeros_like(rows)
    neigh = place(neigh_ref[...])
    live = lax.broadcasted_iota(jnp.int32, (fan, share), 0) < count_ref[...]
    rows[0:fan, 0:share] = jnp.where(live, neigh & 255, -1).astype(F32)
    rows[0:fan, 128 : 128 + share] = (neigh >> 8).astype(F32)
    own = place(self_ref[...])
    rows[fan : fan + 1, 0:share] = (own & 255).astype(F32)
    rows[fan : fan + 1, 128 : 128 + share] = (own >> 8).astype(F32)
    rows[fan + 1 : fan + 2, 0:share] = count_ref[...].astype(F32)
    rows[fan + 2 : fan + 4, 0:pairs] = (pairs_ref[...] & 255).astype(F32)
    rows[fan + 2 : fan + 4, 128 : 128 + pairs] = (pairs_ref[...] >> 8).astype(F32)
    out_ref[0:width, :] = ws_ref[...]
    out_ref[width : 2 * width, :] = wn_ref[...]
    out_ref[2 * width :, :] = rows[...].astype(BF)


def pack(self_two, neigh_two, count_two, pairs, ws, wn, features_t, across):
    width, wide = ws.shape
    operands = (self_two, neigh_two, count_two, pairs, ws, wn, features_t)
    held = [pltpu.VMEM(value.shape, value.dtype) for value in operands[:6]]
    return pl.pallas_call(
        functools.partial(pack_kernel, across),
        out_shape=[
            jax.ShapeDtypeStruct((2 * width + 32, wide), BF),
            jax.ShapeDtypeStruct(features_t.shape, BF),
        ],
        in_specs=[pl.BlockSpec(memory_space=pl.ANY)] * len(operands),
        out_specs=[pl.BlockSpec(memory_space=pltpu.VMEM)] * 2,
        scratch_shapes=[
            *held,
            pltpu.VMEM((32, wide), F32),
            pltpu.SemaphoreType.DMA((len(operands),)),
        ],
        compiler_params=pltpu.CompilerParams(vmem_limit_bytes=16 * 2**20),
        name="pack",
    )(*(in_hbm(value) for value in operands))


def count_blocks(keys_ref, lows_ref, base, out_ref, marks):
    chunks, _, chunk = out_ref.shape
    spans = chunks * chunk // 256
    across = chunk // 256

    def stretch(row, rows):
        small = jnp.broadcast_to(row, (16, 256)).astype(BF)
        return jnp.concatenate([small] * (rows // 16), axis=0)

    def block(pair, _):
        one = jnp.ones((256, 256), BF)
        zero = jnp.zeros((256, 256), BF)
        place = pl.multiple_of(pair * 32, 32)
        rights = []
        for at in (pair * 2, pair * 2 + 1):
            low = stretch(lows_ref[pl.ds(base + at, 1), :], 256)
            rights.append(jnp.where(low == marks[...], one, zero))
        for first in range(0, spans, 16):
            size = min(16, spans - first)
            parts = []
            for side in range(2):
                row = keys_ref[pl.ds(base + pair * 2 + side, 1), :]
                key = stretch(row - float(first * 16), size * 16)
                left = jnp.where(
                    key == marks[0 : size * 16, :], one[: size * 16], zero[: size * 16]
                )
                parts.append(dot(left, rights[side], NT))
            for inner in range(size):
                span = first + inner
                lane = (span % across) * 256
                rows = [part[inner * 16 : (inner + 1) * 16] for part in parts]
                out_ref[span // across, pl.ds(place, 32), lane : lane + 256] = jnp.concatenate(
                    rows, axis=0
                ).astype(out_ref.dtype)
        return 0

    lax.fori_loop(0, 8, block, 0, unroll=8)


def all_marks():
    return lax.broadcasted_iota(jnp.int32, (256, 256), 0).astype(F32).astype(BF)


def count_one_kernel(ids_from, live_from, out_ref, marks, keys, lows, ids_ref, live_ref, sems):
    fan = ids_ref.shape[0]

    @pl.when(pl.program_id(0) == 0)
    def _():
        first = pltpu.make_async_copy(ids_from, ids_ref, sems.at[0])
        other = pltpu.make_async_copy(live_from, live_ref, sems.at[1])
        first.start()
        other.start()
        marks[...] = all_marks()
        first.wait()
        other.wait()
        slots = lax.broadcasted_iota(jnp.int32, (fan, 128), 0)
        high = []
        low = []
        for node in range(16):
            ids = ids_ref[:, node * 128 : (node + 1) * 128]
            live = slots < live_ref[:, node * 128 : (node + 1) * 128]
            high.append(((ids >> 8) * 16 + node).astype(F32))
            low.append(jnp.where(live, ids & 255, -1).astype(F32))
        keys[...] = jnp.concatenate(high, axis=0).T
        lows[...] = jnp.concatenate(low, axis=0).T

    count_blocks(keys, lows, pl.program_id(0) * 16, out_ref, marks)


def count_one_matrix(ids, live, total, chunk):
    fan, nodes = ids.shape
    return pl.pallas_call(
        count_one_kernel,
        grid=(nodes // 256,),
        out_shape=jax.ShapeDtypeStruct((total // chunk, nodes, chunk), F8),
        in_specs=[pl.BlockSpec(memory_space=pl.ANY)] * 2,
        out_specs=pl.BlockSpec((total // chunk, 256, chunk), lambda at: (0, at, 0)),
        scratch_shapes=[
            pltpu.VMEM((256, 256), BF),
            pltpu.VMEM((128, 256), F32),
            pltpu.VMEM((128, 256), F32),
            pltpu.VMEM((fan, nodes), jnp.int32),
            pltpu.VMEM((1, nodes), jnp.int32),
            pltpu.SemaphoreType.DMA((2,)),
        ],
        compiler_params=pltpu.CompilerParams(vmem_limit_bytes=VMEM_LIMIT),
        cost_estimate=pl.CostEstimate(
            flops=2 * nodes * total * 256, bytes_accessed=nodes * total, transcendentals=0
        ),
        name="count_one",
    )(in_hbm(ids), in_hbm(live))


def count_two_kernel(fan, sent_ref, out_ref, marks, keys, lows):
    @pl.when(pl.program_id(0) == 0)
    def _():
        marks[...] = all_marks()
        high = []
        low = []
        for device in range(sent_ref.shape[0]):
            low.append(sent_ref[device, 0:fan, 0:128])
            high.append(sent_ref[device, 0:fan, 128:256] * 16.0 + float(device))
        keys[...] = jnp.concatenate(high, axis=0).T
        lows[...] = jnp.concatenate(low, axis=0).T

    count_blocks(keys, lows, pl.program_id(0) * 16, out_ref, marks)


def count_two_matrix(sent, fan, share, total):
    nodes = sent.shape[0] * share
    return pl.pallas_call(
        functools.partial(count_two_kernel, fan),
        grid=(nodes // 256,),
        out_shape=jax.ShapeDtypeStruct((1, nodes, total), F8),
        in_specs=[pl.BlockSpec(sent.shape, lambda at: (0, 0, 0))],
        out_specs=pl.BlockSpec((1, 256, total), lambda at: (0, at, 0)),
        scratch_shapes=[
            pltpu.VMEM((256, 256), BF),
            pltpu.VMEM((128, 256), F32),
            pltpu.VMEM((128, 256), F32),
        ],
        compiler_params=pltpu.CompilerParams(vmem_limit_bytes=VMEM_LIMIT),
        cost_estimate=pl.CostEstimate(
            flops=2 * nodes * total * 256, bytes_accessed=2 * nodes * total, transcendentals=0
        ),
        name="count_two",
    )(sent)


def hop_kernel(
    steps, self_ref, counts_ref, front_ref, out_ref, table, total, own, up, down, live
):
    owners, width, cap = front_ref.shape
    blocks, _, block = out_ref.shape
    step = pl.program_id(0)
    per = owners // steps
    half = steps // 2
    across = blocks * block // 128

    @pl.when(step == 0)
    def _():
        most = jnp.abs(front_ref[0])
        for owner in range(1, owners):
            most = jnp.maximum(most, jnp.abs(front_ref[owner]))
        most = jnp.max(most.astype(F32), axis=1, keepdims=True)
        power = jnp.ones_like(most)
        back = jnp.ones_like(most)
        for exponent in (32, 32, 16, 16, 8, 4, 2, 1):
            fits = most * power * 2.0**exponent <= 224.0
            power = jnp.where(fits, power * 2.0**exponent, power)
            back = jnp.where(fits, back * 2.0**-exponent, back)
        up[...] = jnp.broadcast_to(power, up.shape)
        down[...] = jnp.broadcast_to(back, down.shape)
        total[...] = jnp.zeros_like(total)
        live[...] = jnp.zeros_like(live)

    def product():
        front = jnp.concatenate([front_ref[step * per + at] for at in range(per)], axis=1)
        front = front.astype(F32) * up[:, 0:1]
        high = front.astype(F8)
        low = ((front - high.astype(F32)) * 16.0).astype(F8)
        ones = jnp.ones((32, front.shape[1]), F8)
        part = dot(jnp.concatenate([high, low, ones], axis=0), counts_ref[0], NT)
        total[...] += part[:width] + part[width : 2 * width] * (1.0 / 16.0)
        live[...] += part[2 * width : 2 * width + 8]

    @pl.when(step < half)
    def _():
        for at in range(owners // half):
            owner = step * (owners // half) + at
            place = pl.multiple_of(owner * cap, cap)
            table[pl.ds(place, cap), 0:width] = front_ref[owner].astype(F32).T
        product()

    @pl.when(step >= half)
    def _():
        for at in range(blocks // half):
            dest = (step - half) * (blocks // half) + at
            for row in range(block):
                place = at * block + row
                node = row % across * 128 + dest * (block // across) + row // across
                own[place : place + 1, :] = table[pl.ds(self_ref[node], 1), :]
            rows = own[at * block : (at + 1) * block, 0:width]
            out_ref[dest, 0:width, :] = rows.T.astype(BF)
        product()

    @pl.when(step == steps - 1)
    def _():
        back = down[:, 0:1]
        inv = 1.0 / live[0:1, :]
        for dest in range(blocks):
            mean = total[:, dest * block : (dest + 1) * block] * back
            mean = mean * inv[:, dest * block : (dest + 1) * block]
            out_ref[dest, width : 2 * width, :] = mean.astype(BF)


def hop(frontier, counts, self_ids, blocks):
    owners, width, cap = frontier.shape
    chunks, nodes, chunk = counts.shape
    block = nodes // blocks
    return pl.pallas_call(
        functools.partial(hop_kernel, chunks),
        grid=(chunks,),
        out_shape=jax.ShapeDtypeStruct((blocks, 2 * width, block), BF),
        in_specs=[
            pl.BlockSpec(memory_space=pltpu.SMEM),
            pl.BlockSpec((1, nodes, chunk), lambda at: (at, 0, 0)),
            pl.BlockSpec((owners, width, cap), lambda at: (0, 0, 0)),
        ],
        out_specs=pl.BlockSpec((blocks, 2 * width, block), lambda at: (0, 0, 0)),
        scratch_shapes=[
            pltpu.VMEM((owners * cap, 128), F32),
            pltpu.VMEM((width, nodes), F32),
            pltpu.VMEM((nodes * 2 // chunks, 128), F32),
            pltpu.VMEM((width, 128), F32),
            pltpu.VMEM((width, 128), F32),
            pltpu.VMEM((8, nodes), F32),
        ],
        compiler_params=pltpu.CompilerParams(vmem_limit_bytes=VMEM_LIMIT),
        cost_estimate=pl.CostEstimate(
            flops=2 * nodes * chunks * chunk * 128,
            bytes_accessed=nodes * chunks * chunk,
            transcendentals=0,
        ),
        name="first_hop",
    )(self_ids, counts, frontier)


def first_kernel(side, me_ref, mine_ref, *refs):
    early_refs, (out_ref, fields_ref) = refs[:side], refs[side:]
    _, depth, block = mine_ref.shape
    row, column = me_ref[0], me_ref[1]
    weights = []
    mine = []
    for far in range(side):
        for near in range(side):
            owner = lax.rem(row + side - far, side) * side + lax.rem(column + side - near, side)
            weights.append(early_refs[far][near, 0:depth, :])
            mine.append(mine_ref[owner])
            fields_ref[owner] = early_refs[far][near, depth:, :].astype(F32)
    pre = dot(jnp.concatenate(weights, axis=0), jnp.concatenate(mine, axis=0), TN)
    hidden = jnp.maximum(pre, 0.0).astype(BF)
    for at in range(out_ref.shape[0]):
        out_ref[at] = hidden


def first(mine, early, me):
    feats, depth, block = mine.shape
    side, rows, wide = early[0].shape
    vm = pl.BlockSpec(memory_space=pltpu.VMEM)
    return pl.pallas_call(
        functools.partial(first_kernel, side),
        out_shape=[
            jax.ShapeDtypeStruct((feats, wide, block), BF),
            jax.ShapeDtypeStruct((feats, rows - depth, wide), F32),
        ],
        in_specs=[pl.BlockSpec(memory_space=pltpu.SMEM)] + [vm] * (1 + side),
        out_specs=[vm, vm],
        compiler_params=pltpu.CompilerParams(vmem_limit_bytes=VMEM_LIMIT),
        name="first_layer",
    )(me, mine, *early)


def mark_rows(ids_ref, out_ref, marks):
    total, count = out_ref.shape
    one = jnp.ones((256, count), BF); zero = jnp.zeros((256, count), BF)
    for first in range(0, total, 256):
        row = jnp.broadcast_to(ids_ref[...] - float(first), (16, count)).astype(BF)
        row = jnp.concatenate([row] * 16, axis=0)
        out_ref[first:first + 256, :] = jnp.where(row == marks, one, zero)

def second_kernel(scale, negative_total, hidden_ref, rows_ref, self_ref, ends_ref, inv_ref, ws_ref, wn_ref, neigh_hbm,
                  out_ref, neigh, own, ends, hidden_t, sem, held):
    copy = pltpu.make_async_copy(neigh_hbm, held, sem)
    copy.start()
    blocks, width, block = hidden_ref.shape
    for at in range(blocks):
        hidden_t[:, at * block:(at + 1) * block] = hidden_ref[at]
    targets = own.shape[1]
    marks = lax.broadcasted_iota(jnp.int32, (256, targets), 0).astype(F32).astype(BF)
    mark_rows(self_ref, own, marks)
    mark_rows(ends_ref, ends, marks)
    inv = inv_ref[...]
    hidden = hidden_t[...]
    hs = dot(hidden, own[...], NN).astype(BF)
    copy.wait()
    neigh[...] = held[...].astype(BF)
    hn = (dot(hidden, neigh[...], NT) * inv).astype(BF)
    embed = (dot(ws_ref[...], hs, TN) + dot(wn_ref[...], hn, TN)).astype(BF)
    rows = dot(embed, ends[...], NN).astype(BF)
    count = rows.shape[1] // 3
    source, dest, negative = rows[:, :count], rows[:, count:2 * count], rows[:, 2 * count:]
    pos = jnp.sum(source.astype(F32) * dest.astype(F32), axis=0, keepdims=True) * scale
    neg = dot(source, negative, TN) * scale
    small = jnp.exp(-jnp.abs(neg))
    neg_sig = jnp.where(neg >= 0, 1.0, small) / (1.0 + small)
    neg_loss = jnp.maximum(neg, 0.0) + jnp.log1p(small)
    small = jnp.exp(-jnp.abs(pos))
    pos_grad = -(jnp.where(pos >= 0, small, 1.0) / (1.0 + small))
    pos_loss = jnp.maximum(-pos, 0.0) + jnp.log1p(small)
    loss = jnp.sum(neg_loss, axis=0, keepdims=True) * (1.0 / negative_total) + pos_loss
    loss = jnp.sum(loss, axis=1, keepdims=True)
    neg_grad = (neg_sig * (1.0 / negative_total)).astype(BF)
    source_grad = (pos_grad * dest.astype(F32) + dot(negative, neg_grad, NT)) * scale
    dest_grad = pos_grad * source.astype(F32) * scale
    negative_grad = dot(source, neg_grad, NN) * scale
    grads = jnp.concatenate([source_grad.astype(BF), dest_grad.astype(BF), negative_grad.astype(BF)], axis=1)
    eg = dot(grads, ends[...], NT).astype(BF)
    groups = out_ref.shape[0]
    many = 2 * ws_ref.shape[0] // groups
    sums = jnp.concatenate([dot(hs, eg, NT), dot(hn, eg, NT)], axis=0).astype(BF)
    for group in range(groups):
        out_ref[group, 0:many, :] = sums[group * many : (group + 1) * many]
    self_back = dot(ws_ref[...], eg, NN).astype(BF)
    neigh_back = (dot(wn_ref[...], eg, NN) * inv).astype(BF)
    hidden_grad = dot(self_back, own[...], NT) + dot(neigh_back, neigh[...], NN)
    pre = jnp.where(hidden > 0, hidden_grad, 0.0).astype(BF)
    rows_one = jnp.concatenate([rows_ref[at] for at in range(blocks)], axis=1)
    part = dot(rows_one, pre, NT)
    few = part.shape[0] // groups
    high = loss.astype(BF).astype(F32)
    mid = (loss - high).astype(BF).astype(F32)
    low = loss - high - mid
    lanes = lax.broadcasted_iota(jnp.int32, (8 - few, part.shape[1]), 1)
    tail = jnp.where(lanes == 0, high, jnp.where(lanes == 1, mid, low))
    for group in range(groups):
        rows = jnp.concatenate([part[group * few : (group + 1) * few], tail], axis=0)
        out_ref[group, many : many + 8, :] = rows.astype(BF)


def second(
    hidden, rows_one, pick_neigh, self_two, ends, inv, ws, wn, scale, negative_total, groups
):
    blocks, width, block = hidden.shape
    nodes = blocks * block
    targets = self_two.shape[1]
    many = ends.shape[1]
    vm = pl.BlockSpec(memory_space=pltpu.VMEM)
    return pl.pallas_call(functools.partial(second_kernel, scale, negative_total),
        out_shape=jax.ShapeDtypeStruct((groups, 2 * width // groups + 8, width), BF),
        in_specs=[vm] * 7 + [pl.BlockSpec(memory_space=pl.ANY)],
        out_specs=vm,
        scratch_shapes=[pltpu.VMEM((targets, nodes), BF), pltpu.VMEM((nodes, targets), BF), pltpu.VMEM((targets, many), BF), pltpu.VMEM((width, nodes), BF), pltpu.SemaphoreType.DMA, pltpu.VMEM((targets, nodes), F8)],
        compiler_params=pltpu.CompilerParams(vmem_limit_bytes=VMEM_LIMIT),
        name="second_layer")(hidden, rows_one, self_two, ends, inv, ws, wn, pick_neigh)

def local(
    features,
    frontier_ids,
    self_one_ids,
    neigh_one_ids,
    count_one,
    self_two_ids,
    neigh_two_ids,
    count_two,
    pos_pairs,
    neg_ids,
    first_self,
    first_neigh,
    second_self,
    second_neigh,
):
    graphs = lax.axis_size("graph")
    feats = lax.axis_size("feat")
    hidden_width = second_self.shape[0]
    scale = 1.0 / math.sqrt(hidden_width)
    negative_total = neg_ids.shape[1]
    nodes = self_one_ids.shape[1]
    fan = neigh_one_ids.shape[1]
    width = features.shape[1]
    cap = frontier_ids.shape[2]
    front = graphs * cap
    share = self_two_ids.shape[1]
    pair_share = pos_pairs.shape[2]

    asked = swap(frontier_ids[0], "graph")

    early, features_t = pack(
        self_two_ids,
        neigh_two_ids[0],
        count_two,
        pos_pairs[0],
        first_self,
        first_neigh,
        features.T,
        nodes // 128,
    )
    side = math.isqrt(feats)
    me = lax.axis_index("feat")
    me = jnp.stack([me // side, me % side]).astype(jnp.int32)
    along = [
        [(at, at // side * side + (at + far) % side) for at in range(feats)]
        for far in range(1, side)
    ]
    across = [
        [(at, (at + far * side) % feats) for at in range(feats)] for far in range(1, side)
    ]
    asked, early = lax.optimization_barrier((asked, early))
    early = jnp.stack([early] + [lax.ppermute(early, "feat", pairs) for pairs in along])
    served = serve(features_t, asked.reshape(-1), graphs, cap)
    one_ids, served, early = lax.optimization_barrier((neigh_one_ids[0], served, early))
    early = [early] + [lax.ppermute(early, "feat", pairs) for pairs in across]
    one_counts = count_one_matrix(one_ids, count_one, front, 2 * cap)
    frontier = swap(served, "graph")
    frontier, early = lax.optimization_barrier((frontier, early))
    rows_one = hop(frontier, one_counts, self_one_ids[0], feats)
    hidden, sent = first(swap(rows_one, "feat"), early, me)
    hidden = swap(hidden, "feat")

    pick_neigh = count_two_matrix(sent, fan, share, nodes)[0]
    self_two = sent[:, fan, :share] + sent[:, fan, 128 : 128 + share] * 256.0
    self_two = self_two.T.reshape(1, -1)
    inv_two = 1.0 / sent[:, fan + 1, :share].T.reshape(1, -1)
    pairs = sent[:, fan + 2 : fan + 4]
    pairs = pairs[:, :, :pair_share] + pairs[:, :, 128 : 128 + pair_share] * 256.0
    pairs = pairs.transpose(1, 0, 2)
    pair_total = feats * pair_share
    ends = jnp.concatenate([pairs.reshape(1, -1).astype(jnp.int32), neg_ids], axis=1)
    ends = (ends % share * feats + ends // share).astype(F32)
    parts = second(
        hidden,
        rows_one,
        pick_neigh,
        self_two,
        ends,
        inv_two,
        second_self,
        second_neigh,
        scale,
        negative_total,
        graphs,
    )

    sums = jnp.sum(swap(parts, "graph").astype(F32), axis=0)
    loss = jnp.sum(sums[-1, 0:3])
    whole = gather_all(sums.astype(BF), "graph").astype(F32)
    second_rows = 2 * hidden_width // graphs
    first_rows = 2 * width // graphs
    second_sums = whole[:, :second_rows].reshape(2 * hidden_width, hidden_width)
    first_sums = whole[:, second_rows : second_rows + first_rows].reshape(-1, hidden_width)
    return (
        first_sums[:width],
        first_sums[width:],
        second_sums[:hidden_width],
        second_sums[hidden_width:],
        loss / (pair_total * graphs),
    )


def solution(mesh):
    placed = (
        P("graph", "feat"),
        P("graph", None, None),
        P("graph", None),
        P("graph", None, None),
        P("graph", None),
        P("graph", "feat"),
        P("graph", None, "feat"),
        P("graph", "feat"),
        P("graph", None, "feat"),
        P("graph", None),
        P("feat", None),
        P("feat", None),
        P(),
        P(),
    )
    return jax.shard_map(
        local,
        mesh=mesh,
        in_specs=placed,
        out_specs=(P("feat", None), P("feat", None), P(), P(), P()),
        check_vma=False,
    )
```

```python
import functools
import math

import jax
import jax.numpy as jnp
from jax import lax
from jax.experimental import pallas as pl
from jax.experimental.pallas import tpu as pltpu
from jax.sharding import PartitionSpec as P

BF = jnp.bfloat16
F32 = jnp.float32
F8 = jnp.float8_e4m3fn
VMEM_LIMIT = 50 * 2**20
NN = ((1,), (0,))
NT = ((1,), (1,))
TN = ((0,), (0,))


def swap(value, axis):
    return lax.all_to_all(value, axis, split_axis=0, concat_axis=0, tiled=True)


def gather_all(value, axis):
    size = lax.axis_size(axis)
    return swap(jnp.broadcast_to(value[None], (size,) + value.shape), axis)


def in_hbm(value):
    return pltpu.with_memory_space_constraint(value, pltpu.HBM)


def dot(former, latter, dims):
    return lax.dot_general(former, latter, (dims, ((), ())), preferred_element_type=F32)


def serve_kernel(ids_ref, feat_ref, out_ref, table, picked):
    width, rows = feat_ref.shape
    groups, _, cap = out_ref.shape
    step = 512

    def fill(at, _):
        at = pl.multiple_of(at * step, step)
        table[pl.ds(at, step), 0:width] = feat_ref[:, pl.ds(at, step)].astype(F32).T
        return 0

    lax.fori_loop(0, rows // step, fill, 0)

    def take(group, side):
        for row in range(0, cap, 8):
            rows = [
                table[pl.ds(ids_ref[group * cap + row + at], 1), :] for at in range(8)
            ]
            picked[side, row : row + 8, :] = jnp.concatenate(rows, axis=0)

    def put(group, side):
        out_ref[group] = picked[side, :, 0:width].T.astype(out_ref.dtype)

    def two(at, _):
        group = at * 2 + 1
        take(group, 1)
        put(group - 1, 0)
        take(group + 1, 0)
        put(group, 1)
        return 0

    take(0, 0)
    lax.fori_loop(0, groups // 2 - 1, two, 0)
    take(groups - 1, 1)
    put(groups - 2, 0)
    put(groups - 1, 1)


def serve(features_t, ids, groups, cap):
    width, rows = features_t.shape
    return pl.pallas_call(
        serve_kernel,
        out_shape=jax.ShapeDtypeStruct((groups, width, cap), features_t.dtype),
        in_specs=[
            pl.BlockSpec(memory_space=pltpu.SMEM),
            pl.BlockSpec(memory_space=pltpu.VMEM),
        ],
        out_specs=pl.BlockSpec(memory_space=pltpu.VMEM),
        scratch_shapes=[pltpu.VMEM((rows, 128), F32), pltpu.VMEM((2, cap, 128), F32)],
        compiler_params=pltpu.CompilerParams(vmem_limit_bytes=VMEM_LIMIT),
        name="serve",
    )(ids, features_t)


def pack_kernel(across, *refs):
    sources, (out_ref, copy_ref), held, rows, sems = refs[:7], refs[7:9], refs[9:15], refs[15], refs[16]
    copies = [
        pltpu.make_async_copy(source, place, sems.at[at])
        for at, (source, place) in enumerate(zip(sources, [*held, copy_ref]))
    ]
    for copy in copies:
        copy.start()
    for copy in copies:
        copy.wait()
    self_ref, neigh_ref, count_ref, pairs_ref, ws_ref, wn_ref = held
    width = ws_ref.shape[0]
    fan, share = neigh_ref.shape
    pairs = pairs_ref.shape[1]

    def place(ids):
        return (ids & 127) * across + (ids >> 7)

    rows[...] = jnp.zeros_like(rows)
    neigh = place(neigh_ref[...])
    live = lax.broadcasted_iota(jnp.int32, (fan, share), 0) < count_ref[...]
    rows[0:fan, 0:share] = jnp.where(live, neigh & 255, -1).astype(F32)
    rows[0:fan, 128 : 128 + share] = (neigh >> 8).astype(F32)
    own = place(self_ref[...])
    rows[fan : fan + 1, 0:share] = (own & 255).astype(F32)
    rows[fan : fan + 1, 128 : 128 + share] = (own >> 8).astype(F32)
    rows[fan + 1 : fan + 2, 0:share] = count_ref[...].astype(F32)
    rows[fan + 2 : fan + 4, 0:pairs] = (pairs_ref[...] & 255).astype(F32)
    rows[fan + 2 : fan + 4, 128 : 128 + pairs] = (pairs_ref[...] >> 8).astype(F32)
    out_ref[0:width, :] = ws_ref[...]
    out_ref[width : 2 * width, :] = wn_ref[...]
    out_ref[2 * width :, :] = rows[...].astype(BF)


def pack(self_two, neigh_two, count_two, pairs, ws, wn, features_t, across):
    width, wide = ws.shape
    operands = (self_two, neigh_two, count_two, pairs, ws, wn, features_t)
    held = [pltpu.VMEM(value.shape, value.dtype) for value in operands[:6]]
    return pl.pallas_call(
        functools.partial(pack_kernel, across),
        out_shape=[
            jax.ShapeDtypeStruct((2 * width + 32, wide), BF),
            jax.ShapeDtypeStruct(features_t.shape, BF),
        ],
        in_specs=[pl.BlockSpec(memory_space=pl.ANY)] * len(operands),
        out_specs=[pl.BlockSpec(memory_space=pltpu.VMEM)] * 2,
        scratch_shapes=[
            *held,
            pltpu.VMEM((32, wide), F32),
            pltpu.SemaphoreType.DMA((len(operands),)),
        ],
        compiler_params=pltpu.CompilerParams(vmem_limit_bytes=16 * 2**20),
        name="pack",
    )(*(in_hbm(value) for value in operands))


def count_blocks(keys_ref, lows_ref, base, out_ref, marks):
    chunks, _, chunk = out_ref.shape
    spans = chunks * chunk // 256
    across = chunk // 256

    def stretch(row, rows):
        small = jnp.broadcast_to(row, (16, 256)).astype(BF)
        return jnp.concatenate([small] * (rows // 16), axis=0)

    def block(pair, _):
        one = jnp.ones((256, 256), BF)
        zero = jnp.zeros((256, 256), BF)
        place = pl.multiple_of(pair * 32, 32)
        rights = []
        for at in (pair * 2, pair * 2 + 1):
            low = stretch(lows_ref[pl.ds(base + at, 1), :], 256)
            rights.append(jnp.where(low == marks[...], one, zero))
        for first in range(0, spans, 16):
            size = min(16, spans - first)
            parts = []
            for side in range(2):
                row = keys_ref[pl.ds(base + pair * 2 + side, 1), :]
                key = stretch(row - float(first * 16), size * 16)
                left = jnp.where(
                    key == marks[0 : size * 16, :], one[: size * 16], zero[: size * 16]
                )
                parts.append(dot(left, rights[side], NT))
            for inner in range(size):
                span = first + inner
                lane = (span % across) * 256
                rows = [part[inner * 16 : (inner + 1) * 16] for part in parts]
                out_ref[span // across, pl.ds(place, 32), lane : lane + 256] = jnp.concatenate(
                    rows, axis=0
                ).astype(out_ref.dtype)
        return 0

    lax.fori_loop(0, 8, block, 0, unroll=8)


def all_marks():
    return lax.broadcasted_iota(jnp.int32, (256, 256), 0).astype(F32).astype(BF)


def count_one_kernel(ids_from, live_from, out_ref, done_ref, marks, keys, lows, ids_ref, live_ref, sems):
    fan = ids_ref.shape[0]

    @pl.when(pl.program_id(0) == 0)
    def _():
        first = pltpu.make_async_copy(ids_from, ids_ref, sems.at[0])
        other = pltpu.make_async_copy(live_from, live_ref, sems.at[1])
        first.start()
        other.start()
        marks[...] = all_marks()
        first.wait()
        other.wait()
        done_ref[...] = jnp.zeros_like(done_ref)
        slots = lax.broadcasted_iota(jnp.int32, (fan, 128), 0)
        high = []
        low = []
        for node in range(16):
            ids = ids_ref[:, node * 128 : (node + 1) * 128]
            live = slots < live_ref[:, node * 128 : (node + 1) * 128]
            high.append(((ids >> 8) * 16 + node).astype(F32))
            low.append(jnp.where(live, ids & 255, -1).astype(F32))
        keys[...] = jnp.concatenate(high, axis=0).T
        lows[...] = jnp.concatenate(low, axis=0).T

    count_blocks(keys, lows, pl.program_id(0) * 16, out_ref, marks)


def count_one_matrix(ids, live, total, chunk):
    fan, nodes = ids.shape
    return pl.pallas_call(
        count_one_kernel,
        grid=(nodes // 256,),
        out_shape=[
            jax.ShapeDtypeStruct((total // chunk, nodes, chunk), F8),
            jax.ShapeDtypeStruct((8, 128), F32),
        ],
        in_specs=[pl.BlockSpec(memory_space=pl.ANY)] * 2,
        out_specs=[
            pl.BlockSpec((total // chunk, 256, chunk), lambda at: (0, at, 0)),
            pl.BlockSpec((8, 128), lambda at: (0, 0)),
        ],
        scratch_shapes=[
            pltpu.VMEM((256, 256), BF),
            pltpu.VMEM((128, 256), F32),
            pltpu.VMEM((128, 256), F32),
            pltpu.VMEM((fan, nodes), jnp.int32),
            pltpu.VMEM((1, nodes), jnp.int32),
            pltpu.SemaphoreType.DMA((2,)),
        ],
        compiler_params=pltpu.CompilerParams(vmem_limit_bytes=VMEM_LIMIT),
        cost_estimate=pl.CostEstimate(
            flops=2 * nodes * total * 256, bytes_accessed=nodes * total, transcendentals=0
        ),
        name="count_one",
    )(in_hbm(ids), in_hbm(live))


def count_two_kernel(fan, sent_ref, out_ref, marks, keys, lows):
    @pl.when(pl.program_id(0) == 0)
    def _():
        marks[...] = all_marks()
        high = []
        low = []
        for device in range(sent_ref.shape[0]):
            low.append(sent_ref[device, 0:fan, 0:128])
            high.append(sent_ref[device, 0:fan, 128:256] * 16.0 + float(device))
        keys[...] = jnp.concatenate(high, axis=0).T
        lows[...] = jnp.concatenate(low, axis=0).T

    count_blocks(keys, lows, pl.program_id(0) * 16, out_ref, marks)


def count_two_matrix(sent, fan, share, total):
    nodes = sent.shape[0] * share
    return pl.pallas_call(
        functools.partial(count_two_kernel, fan),
        grid=(nodes // 256,),
        out_shape=jax.ShapeDtypeStruct((1, nodes, total), F8),
        in_specs=[pl.BlockSpec(sent.shape, lambda at: (0, 0, 0))],
        out_specs=pl.BlockSpec((1, 256, total), lambda at: (0, at, 0)),
        scratch_shapes=[
            pltpu.VMEM((256, 256), BF),
            pltpu.VMEM((128, 256), F32),
            pltpu.VMEM((128, 256), F32),
        ],
        compiler_params=pltpu.CompilerParams(vmem_limit_bytes=VMEM_LIMIT),
        cost_estimate=pl.CostEstimate(
            flops=2 * nodes * total * 256, bytes_accessed=2 * nodes * total, transcendentals=0
        ),
        name="count_two",
    )(sent)


def hop_kernel(
    steps, self_ref, counts_ref, front_ref, out_ref, table, total, own, up, down, live
):
    owners, width, cap = front_ref.shape
    blocks, _, block = out_ref.shape
    step = pl.program_id(0)
    per = owners // steps
    half = steps // 2
    across = blocks * block // 128

    @pl.when(step == 0)
    def _():
        most = jnp.abs(front_ref[0])
        for owner in range(1, owners):
            most = jnp.maximum(most, jnp.abs(front_ref[owner]))
        most = jnp.max(most.astype(F32), axis=1, keepdims=True)
        power = jnp.ones_like(most)
        back = jnp.ones_like(most)
        for exponent in (32, 32, 16, 16, 8, 4, 2, 1):
            fits = most * power * 2.0**exponent <= 224.0
            power = jnp.where(fits, power * 2.0**exponent, power)
            back = jnp.where(fits, back * 2.0**-exponent, back)
        up[...] = jnp.broadcast_to(power, up.shape)
        down[...] = jnp.broadcast_to(back, down.shape)
        total[...] = jnp.zeros_like(total)
        live[...] = jnp.zeros_like(live)

    def product():
        front = jnp.concatenate([front_ref[step * per + at] for at in range(per)], axis=1)
        front = front.astype(F32) * up[:, 0:1]
        high = front.astype(F8)
        low = ((front - high.astype(F32)) * 16.0).astype(F8)
        ones = jnp.ones((32, front.shape[1]), F8)
        part = dot(jnp.concatenate([high, low, ones], axis=0), counts_ref[0], NT)
        total[...] += part[:width] + part[width : 2 * width] * (1.0 / 16.0)
        live[...] += part[2 * width : 2 * width + 8]

    @pl.when(step < half)
    def _():
        for at in range(owners // half):
            owner = step * (owners // half) + at
            place = pl.multiple_of(owner * cap, cap)
            table[pl.ds(place, cap), 0:width] = front_ref[owner].astype(F32).T
        product()

    @pl.when(step >= half)
    def _():
        for at in range(blocks // half):
            dest = (step - half) * (blocks // half) + at
            for row in range(block):
                place = at * block + row
                node = row % across * 128 + dest * (block // across) + row // across
                own[place : place + 1, :] = table[pl.ds(self_ref[node], 1), :]
            rows = own[at * block : (at + 1) * block, 0:width]
            out_ref[dest, 0:width, :] = rows.T.astype(BF)
        product()

    @pl.when(step == steps - 1)
    def _():
        back = down[:, 0:1]
        inv = 1.0 / live[0:1, :]
        for dest in range(blocks):
            mean = total[:, dest * block : (dest + 1) * block] * back
            mean = mean * inv[:, dest * block : (dest + 1) * block]
            out_ref[dest, width : 2 * width, :] = mean.astype(BF)


def hop(frontier, counts, self_ids, blocks):
    owners, width, cap = frontier.shape
    chunks, nodes, chunk = counts.shape
    block = nodes // blocks
    return pl.pallas_call(
        functools.partial(hop_kernel, chunks),
        grid=(chunks,),
        out_shape=jax.ShapeDtypeStruct((blocks, 2 * width, block), BF),
        in_specs=[
            pl.BlockSpec(memory_space=pltpu.SMEM),
            pl.BlockSpec((1, nodes, chunk), lambda at: (at, 0, 0)),
            pl.BlockSpec((owners, width, cap), lambda at: (0, 0, 0)),
        ],
        out_specs=pl.BlockSpec((blocks, 2 * width, block), lambda at: (0, 0, 0)),
        scratch_shapes=[
            pltpu.VMEM((owners * cap, 128), F32),
            pltpu.VMEM((width, nodes), F32),
            pltpu.VMEM((nodes * 2 // chunks, 128), F32),
            pltpu.VMEM((width, 128), F32),
            pltpu.VMEM((width, 128), F32),
            pltpu.VMEM((8, nodes), F32),
        ],
        compiler_params=pltpu.CompilerParams(vmem_limit_bytes=VMEM_LIMIT),
        cost_estimate=pl.CostEstimate(
            flops=2 * nodes * chunks * chunk * 128,
            bytes_accessed=nodes * chunks * chunk,
            transcendentals=0,
        ),
        name="first_hop",
    )(self_ids, counts, frontier)


def first_kernel(side, me_ref, mine_ref, *refs):
    early_refs, (out_ref, fields_ref) = refs[:side], refs[side:]
    _, depth, block = mine_ref.shape
    row, column = me_ref[0], me_ref[1]
    weights = []
    mine = []
    for far in range(side):
        for near in range(side):
            owner = lax.rem(row + side - far, side) * side + lax.rem(column + side - near, side)
            weights.append(early_refs[far][near, 0:depth, :])
            mine.append(mine_ref[owner])
            fields_ref[owner] = early_refs[far][near, depth:, :].astype(F32)
    pre = dot(jnp.concatenate(weights, axis=0), jnp.concatenate(mine, axis=0), TN)
    hidden = jnp.maximum(pre, 0.0).astype(BF)
    for at in range(out_ref.shape[0]):
        out_ref[at] = hidden


def first(mine, early, me):
    feats, depth, block = mine.shape
    side, rows, wide = early[0].shape
    vm = pl.BlockSpec(memory_space=pltpu.VMEM)
    return pl.pallas_call(
        functools.partial(first_kernel, side),
        out_shape=[
            jax.ShapeDtypeStruct((feats, wide, block), BF),
            jax.ShapeDtypeStruct((feats, rows - depth, wide), F32),
        ],
        in_specs=[pl.BlockSpec(memory_space=pltpu.SMEM)] + [vm] * (1 + side),
        out_specs=[vm, vm],
        compiler_params=pltpu.CompilerParams(vmem_limit_bytes=VMEM_LIMIT),
        name="first_layer",
    )(me, mine, *early)


def mark_rows(ids_ref, out_ref, marks):
    total, count = out_ref.shape
    one = jnp.ones((256, count), BF); zero = jnp.zeros((256, count), BF)
    for first in range(0, total, 256):
        row = jnp.broadcast_to(ids_ref[...] - float(first), (16, count)).astype(BF)
        row = jnp.concatenate([row] * 16, axis=0)
        out_ref[first:first + 256, :] = jnp.where(row == marks, one, zero)

def second_kernel(scale, negative_total, hidden_ref, rows_ref, self_ref, ends_ref, inv_ref, ws_ref, wn_ref, neigh_hbm,
                  out_ref, neigh, own, ends, hidden_t, sem, held):
    copy = pltpu.make_async_copy(neigh_hbm, held, sem)
    copy.start()
    blocks, width, block = hidden_ref.shape
    for at in range(blocks):
        hidden_t[:, at * block:(at + 1) * block] = hidden_ref[at]
    targets = own.shape[1]
    marks = lax.broadcasted_iota(jnp.int32, (256, targets), 0).astype(F32).astype(BF)
    mark_rows(self_ref, own, marks)
    mark_rows(ends_ref, ends, marks)
    inv = inv_ref[...]
    hidden = hidden_t[...]
    hs = dot(hidden, own[...], NN).astype(BF)
    copy.wait()
    neigh[...] = held[...].astype(BF)
    hn = (dot(hidden, neigh[...], NT) * inv).astype(BF)
    embed = (dot(ws_ref[...], hs, TN) + dot(wn_ref[...], hn, TN)).astype(BF)
    rows = dot(embed, ends[...], NN).astype(BF)
    count = rows.shape[1] // 3
    source, dest, negative = rows[:, :count], rows[:, count:2 * count], rows[:, 2 * count:]
    pos = jnp.sum(source.astype(F32) * dest.astype(F32), axis=0, keepdims=True) * scale
    neg = dot(source, negative, TN) * scale
    small = jnp.exp(-jnp.abs(neg))
    neg_sig = jnp.where(neg >= 0, 1.0, small) / (1.0 + small)
    neg_loss = jnp.maximum(neg, 0.0) + jnp.log1p(small)
    small = jnp.exp(-jnp.abs(pos))
    pos_grad = -(jnp.where(pos >= 0, small, 1.0) / (1.0 + small))
    pos_loss = jnp.maximum(-pos, 0.0) + jnp.log1p(small)
    loss = jnp.sum(neg_loss, axis=0, keepdims=True) * (1.0 / negative_total) + pos_loss
    loss = jnp.sum(loss, axis=1, keepdims=True)
    neg_grad = (neg_sig * (1.0 / negative_total)).astype(BF)
    source_grad = (pos_grad * dest.astype(F32) + dot(negative, neg_grad, NT)) * scale
    dest_grad = pos_grad * source.astype(F32) * scale
    negative_grad = dot(source, neg_grad, NN) * scale
    grads = jnp.concatenate([source_grad.astype(BF), dest_grad.astype(BF), negative_grad.astype(BF)], axis=1)
    eg = dot(grads, ends[...], NT).astype(BF)
    groups = out_ref.shape[0]
    many = 2 * ws_ref.shape[0] // groups
    sums = jnp.concatenate([dot(hs, eg, NT), dot(hn, eg, NT)], axis=0).astype(BF)
    for group in range(groups):
        out_ref[group, 0:many, :] = sums[group * many : (group + 1) * many]
    self_back = dot(ws_ref[...], eg, NN).astype(BF)
    neigh_back = (dot(wn_ref[...], eg, NN) * inv).astype(BF)
    hidden_grad = dot(self_back, own[...], NT) + dot(neigh_back, neigh[...], NN)
    pre = jnp.where(hidden > 0, hidden_grad, 0.0).astype(BF)
    rows_one = jnp.concatenate([rows_ref[at] for at in range(blocks)], axis=1)
    part = dot(rows_one, pre, NT)
    few = part.shape[0] // groups
    high = loss.astype(BF).astype(F32)
    mid = (loss - high).astype(BF).astype(F32)
    low = loss - high - mid
    lanes = lax.broadcasted_iota(jnp.int32, (8 - few, part.shape[1]), 1)
    tail = jnp.where(lanes == 0, high, jnp.where(lanes == 1, mid, low))
    for group in range(groups):
        rows = jnp.concatenate([part[group * few : (group + 1) * few], tail], axis=0)
        out_ref[group, many : many + 8, :] = rows.astype(BF)


def second(
    hidden, rows_one, pick_neigh, self_two, ends, inv, ws, wn, scale, negative_total, groups
):
    blocks, width, block = hidden.shape
    nodes = blocks * block
    targets = self_two.shape[1]
    many = ends.shape[1]
    vm = pl.BlockSpec(memory_space=pltpu.VMEM)
    return pl.pallas_call(functools.partial(second_kernel, scale, negative_total),
        out_shape=jax.ShapeDtypeStruct((groups, 2 * width // groups + 8, width), BF),
        in_specs=[vm] * 7 + [pl.BlockSpec(memory_space=pl.ANY)],
        out_specs=vm,
        scratch_shapes=[pltpu.VMEM((targets, nodes), BF), pltpu.VMEM((nodes, targets), BF), pltpu.VMEM((targets, many), BF), pltpu.VMEM((width, nodes), BF), pltpu.SemaphoreType.DMA, pltpu.VMEM((targets, nodes), F8)],
        compiler_params=pltpu.CompilerParams(vmem_limit_bytes=VMEM_LIMIT),
        name="second_layer")(hidden, rows_one, self_two, ends, inv, ws, wn, pick_neigh)

def local(
    features,
    frontier_ids,
    self_one_ids,
    neigh_one_ids,
    count_one,
    self_two_ids,
    neigh_two_ids,
    count_two,
    pos_pairs,
    neg_ids,
    first_self,
    first_neigh,
    second_self,
    second_neigh,
):
    graphs = lax.axis_size("graph")
    feats = lax.axis_size("feat")
    hidden_width = second_self.shape[0]
    scale = 1.0 / math.sqrt(hidden_width)
    negative_total = neg_ids.shape[1]
    nodes = self_one_ids.shape[1]
    fan = neigh_one_ids.shape[1]
    width = features.shape[1]
    cap = frontier_ids.shape[2]
    front = graphs * cap
    share = self_two_ids.shape[1]
    pair_share = pos_pairs.shape[2]

    asked = swap(frontier_ids[0], "graph")

    early, features_t = pack(
        self_two_ids,
        neigh_two_ids[0],
        count_two,
        pos_pairs[0],
        first_self,
        first_neigh,
        features.T,
        nodes // 128,
    )
    side = math.isqrt(feats)
    me = lax.axis_index("feat")
    me = jnp.stack([me // side, me % side]).astype(jnp.int32)
    along = [
        [(at, at // side * side + (at + far) % side) for at in range(feats)]
        for far in range(1, side)
    ]
    across = [
        [(at, (at + far * side) % feats) for at in range(feats)] for far in range(1, side)
    ]
    served = serve(features_t, asked.reshape(-1), graphs, cap)
    one_ids, served, early = lax.optimization_barrier((neigh_one_ids[0], served, early))
    early = jnp.stack([early] + [lax.ppermute(early, "feat", pairs) for pairs in along])
    one_counts, done = count_one_matrix(one_ids, count_one, front, 2 * cap)
    early, done = lax.optimization_barrier((early, done))
    me = me + done[0, :2].astype(jnp.int32)
    early = [early] + [lax.ppermute(early, "feat", pairs) for pairs in across]
    frontier = swap(served, "graph")
    frontier, early = lax.optimization_barrier((frontier, early))
    rows_one = hop(frontier, one_counts, self_one_ids[0], feats)
    hidden, sent = first(swap(rows_one, "feat"), early, me)
    hidden = swap(hidden, "feat")

    pick_neigh = count_two_matrix(sent, fan, share, nodes)[0]
    self_two = sent[:, fan, :share] + sent[:, fan, 128 : 128 + share] * 256.0
    self_two = self_two.T.reshape(1, -1)
    inv_two = 1.0 / sent[:, fan + 1, :share].T.reshape(1, -1)
    pairs = sent[:, fan + 2 : fan + 4]
    pairs = pairs[:, :, :pair_share] + pairs[:, :, 128 : 128 + pair_share] * 256.0
    pairs = pairs.transpose(1, 0, 2)
    pair_total = feats * pair_share
    ends = jnp.concatenate([pairs.reshape(1, -1).astype(jnp.int32), neg_ids], axis=1)
    ends = (ends % share * feats + ends // share).astype(F32)
    parts = second(
        hidden,
        rows_one,
        pick_neigh,
        self_two,
        ends,
        inv_two,
        second_self,
        second_neigh,
        scale,
        negative_total,
        graphs,
    )

    sums = jnp.sum(swap(parts, "graph").astype(F32), axis=0)
    loss = jnp.sum(sums[-1, 0:3])
    whole = gather_all(sums.astype(BF), "graph").astype(F32)
    second_rows = 2 * hidden_width // graphs
    first_rows = 2 * width // graphs
    second_sums = whole[:, :second_rows].reshape(2 * hidden_width, hidden_width)
    first_sums = whole[:, second_rows : second_rows + first_rows].reshape(-1, hidden_width)
    return (
        first_sums[:width],
        first_sums[width:],
        second_sums[:hidden_width],
        second_sums[hidden_width:],
        loss / (pair_total * graphs),
    )


def solution(mesh):
    placed = (
        P("graph", "feat"),
        P("graph", None, None),
        P("graph", None),
        P("graph", None, None),
        P("graph", None),
        P("graph", "feat"),
        P("graph", None, "feat"),
        P("graph", "feat"),
        P("graph", None, "feat"),
        P("graph", None),
        P("feat", None),
        P("feat", None),
        P(),
        P(),
    )
    return jax.shard_map(
        local,
        mesh=mesh,
        in_specs=placed,
        out_specs=(P("feat", None), P("feat", None), P(), P(), P()),
        check_vma=False,
    )
```
